32 devices in a mesh: kgrp: 4 (over x, core), band: 8 (over z, y).
Axes of the slice: x: 2, y: 2, z: 4, core: 2. Of those that a mesh axis runs over, the one named last changes fastest.
Arguments:
- orbitals: bfloat16 [4, 128, 2, 32768], P('kgrp', 'band'), may hold values from -6 to 6
- points: int32 [512], replicated, may hold values from 0 to 32767, as said below
- partner: int32 [4], replicated, may hold values from 0 to 3, each once
- coulomb: bfloat16 [512, 32768], P(None, 'band'), may hold values from -0.01171875 to 0.01171875
Outputs:
- exchange_term: bfloat16 [4, 128, 2, 32768], P('kgrp', 'band')
The draws below stay inside these ranges and needn't reach their ends.
Inputs may be any that keep to these rules, and one draw needn't show every extreme that they name: `points`: 512 distinct grid cells; cells 0 and 32767 are always among them.
All inputs are finite; a program needn't handle non-finite values.
Results may differ from the reference program's by a relative error of at most 0.0057.
Values may be sent and summed in bfloat16 or wider, within the bound.
No kernel may reach another device: no remote copies, remote signals or barrier semaphores. Data moves between devices by JAX's collectives and lax.ppermute only.
A program may use at most 128 MiB of HBM per device.

```python
import jax
import jax.numpy as jnp
from jax import lax

NB = 128
GX = 32
GY = 32
GZ = 32
NU = 512
NKG = 4
NG = 32768


def draw_points(key, part):
    first_key, second_key = jax.random.split(jax.random.fold_in(key, 17))
    inner = jax.random.permutation(first_key, NG - 2)[:NU - 2] + 1
    base = jnp.concatenate([jnp.zeros((1,), jnp.int32), inner.astype(jnp.int32), jnp.full((1,), NG - 1, jnp.int32)])
    order = jax.random.permutation(second_key, NU)
    return base[order].astype(jnp.int32)


def level_of(key, extent, cuts, smallest, largest):
    loudness = 1.0
    for dim, parts in cuts:
        steps = jax.random.uniform(jax.random.fold_in(jax.random.fold_in(key, 6), dim), (parts,), jnp.float32, smallest / len(cuts), largest / len(cuts))
        loudness = loudness * jnp.repeat(jnp.exp(steps), extent[dim] // parts).reshape((-1,) + (1,) * (len(extent) - 1 - dim))
    return loudness


def normal_values(stream_key, extent, scale, reach, cuts=(), held_as=jnp.bfloat16):
    array = jax.random.normal(stream_key, extent, jnp.float32) * scale
    if len(cuts) > 0:
        array = level_of(stream_key, extent, cuts, -0.22, 0.18) * array
    return jnp.clip(array, min=-reach, max=reach).astype(held_as)


def setup_inputs(seed: int = 0) -> dict:
    splits = jax.random.split(jax.random.key(seed), 5)
    return {
        "orbitals": normal_values(splits[0], (NKG, NB, 2, NG), 1.0, 6.0, ((0, 4), (1, 8))),
        "points": draw_points(jax.random.fold_in(splits[4], 71), 0),
        "partner": jax.random.permutation(splits[2], NKG).astype(jnp.int32),
        "coulomb": normal_values(splits[3], (NU, NG), (4 * NB * NU) ** -0.5, 0.01171875, ((1, 8),)),
    }


def reference(orbitals, points, partner, coulomb):
    values = jnp.take(orbitals, points, axis=3)
    groups = jnp.arange(NKG, dtype=jnp.int32)
    source = jnp.zeros((NKG,), jnp.int32).at[partner].set(groups)
    coul_f = coulomb.astype(jnp.float32)

    def per_group(group):
        orbital = orbitals[group].astype(jnp.float32)
        own_vals = values[group].astype(jnp.float32)
        src_vals = values[source[group]].astype(jnp.float32)
        turned = jnp.stack([-own_vals[:, 1], own_vals[:, 0]], axis=1)
        own_coef = jnp.stack([own_vals, turned], axis=2)
        density = jnp.einsum('icqm,icr->qmr', own_coef, orbital)
        weighted = (coul_f[None] * density).astype(jnp.bfloat16).astype(jnp.float32)
        src_re = src_vals[:, 0]
        src_im = src_vals[:, 1]
        src_coef = -jnp.stack([jnp.stack([src_re, -src_im], axis=1), jnp.stack([src_im, src_re], axis=1)], axis=1)
        on_grid = jnp.einsum('ipqm,qmr->ipr', src_coef, weighted).astype(jnp.bfloat16).astype(jnp.float32)
        complex_grid = lax.complex(on_grid[:, 0], on_grid[:, 1]).reshape(NB, GX, GY, GZ)
        spectrum = jnp.fft.fftn(complex_grid, axes=(1, 2, 3), norm="ortho").reshape(NB, NG)
        return jnp.stack([jnp.real(spectrum), jnp.imag(spectrum)], axis=1).astype(jnp.bfloat16)

    return lax.map(per_group, groups)
```

```python
import math

import jax
import jax.numpy as jnp
import numpy as np
from jax import lax
from jax.experimental import pallas as pl
from jax.experimental.pallas import tpu as pltpu
from jax.sharding import PartitionSpec as P

GX = 32
GY = 32
GZ = 32
LANES = 128
BF16 = jnp.bfloat16
F32 = jnp.float32
VMEM_BYTES = 56 * 1024 * 1024


def round_bf16(values):
    return values.astype(BF16).astype(np.float64)


def table_scale(length):
    cosines = np.cos(2.0 * np.pi * np.arange(length // 4) / length)
    best = (np.inf, 1.0)
    for scale in np.linspace(1.0, 2.0, 8193)[:-1]:
        exact = scale * cosines
        error = float(np.max(np.abs(round_bf16(exact) / exact - 1.0)))
        best = min(best, (error, float(scale)))
    return best[1]


def plane_table(scale):
    cell = np.arange(GY * GZ)
    y, z = cell // GZ, cell % GZ
    turns = (y[:, None] * y[None, :] % GY) / GY + (z[:, None] * z[None, :] % GZ) / GZ
    angle = 2.0 * np.pi * (turns % 1.0)
    return (scale * np.stack([np.cos(angle), np.sin(angle)])).astype(BF16)


def line_table(scale, order, planes, bands):
    count = len(order)
    device = np.arange(count)[:, None, None]
    plane = np.arange(planes)[None, :, None]
    x = planes * (device ^ np.array(order)[None, None, :]) + plane
    kx = np.arange(GX)[None, :, None, None]
    angle = 2.0 * np.pi * (kx * x[:, None] % GX) / GX
    cos_t, sin_t = np.cos(angle), np.sin(angle)
    pair = np.stack([np.stack([cos_t, sin_t], -1), np.stack([-sin_t, cos_t], -1)], 2)
    table = np.zeros((count, bands, GX, 2, planes, count, bands, 2), np.float64)
    for band in range(bands):
        table[:, band, :, :, :, :, band, :] = pair
    return (scale * table).reshape(count, bands * GX * 2, planes * count * bands * 2).astype(BF16)


def turn_table(rows):
    table = np.zeros((rows, rows), np.float32)
    even = np.arange(0, rows, 2)
    table[even, even + 1] = -1.0
    table[even + 1, even] = 1.0
    return table.astype(BF16)


def dot(a, b):
    return jnp.dot(a, b, preferred_element_type=F32)


def pick_kernel(points_ref, tiles_ref, out_ref):
    rows = tiles_ref.shape[1]
    lane = lax.broadcasted_iota(jnp.int32, (rows, LANES), 1)

    @pl.loop(0, out_ref.shape[0])
    def _(group):
        def step(m, total):
            point = points_ref[group * LANES + m]
            tile = tiles_ref[point // LANES].astype(F32)
            shift = (m - point % LANES + LANES) % LANES
            return jnp.where(lane == m, pltpu.roll(tile, shift, 1), total)

        total = lax.fori_loop(0, LANES, step, jnp.zeros((rows, LANES), F32), unroll=8)
        out_ref[group] = total.astype(BF16)


def pick(tiles, points):
    groups = points.shape[0] // LANES
    rows = tiles.shape[1]
    out = pl.pallas_call(
        pick_kernel,
        in_specs=[pl.BlockSpec(memory_space=pltpu.SMEM), pl.BlockSpec(memory_space=pltpu.VMEM)],
        out_specs=pl.BlockSpec(memory_space=pltpu.VMEM),
        out_shape=jax.ShapeDtypeStruct((groups, rows, LANES), BF16),
        compiler_params=pltpu.CompilerParams(vmem_limit_bytes=VMEM_BYTES),
        name="pick_points",
    )(points, tiles)
    return out.transpose(1, 0, 2).reshape(rows, groups * LANES)


def coef_kernel(both_ref, turn_ref, own_ref, src_ref):
    count, _, rows, nu = both_ref.shape
    own = jnp.concatenate([both_ref[k, 0] for k in range(count)], axis=0)
    src = jnp.concatenate([both_ref[k, 1] for k in range(count)], axis=0)
    turn = turn_ref[...]
    own_ref[:nu] = own.astype(F32).T.astype(BF16)
    own_ref[nu:] = dot(turn, own).T.astype(BF16)
    src_ref[:, :nu] = -src
    src_ref[:, nu:] = (-dot(turn, src)).astype(BF16)


def coefficients(both, turn):
    count, _, rows, nu = both.shape
    return pl.pallas_call(
        coef_kernel,
        out_shape=(
            jax.ShapeDtypeStruct((2 * nu, count * rows), BF16),
            jax.ShapeDtypeStruct((count * rows, 2 * nu), BF16),
        ),
        compiler_params=pltpu.CompilerParams(vmem_limit_bytes=VMEM_BYTES),
        name="coefficients",
    )(both, turn)


def exchange_kernel(count, *refs):
    cells = refs[:count]
    own_ref, src_ref, coulomb_ref, table_ref, turn_ref = refs[count : count + 5]
    outs = refs[count + 5 : 2 * count + 5]
    grid_ref = refs[2 * count + 5]
    nu = coulomb_ref.shape[0]
    rows = cells[0].shape[1]
    wide = 2 * LANES
    for part in range(GY * GZ // wide):
        columns = slice(part * wide, (part + 1) * wide)
        tiles = [
            jnp.concatenate([c[2 * part + t] for c in cells], axis=0) for t in range(2)
        ]
        density = dot(own_ref[...], jnp.concatenate(tiles, axis=1))
        coulomb = coulomb_ref[:, columns].astype(F32)
        weighted = jnp.concatenate(
            [(coulomb * density[:nu]).astype(BF16), (coulomb * density[nu:]).astype(BF16)], axis=0
        )
        grid_ref[:, columns] = dot(src_ref[...], weighted).astype(BF16)
    field = grid_ref[...]
    turned = (-dot(turn_ref[...], field)).astype(BF16)
    plane = (dot(field, table_ref[0]) + dot(turned, table_ref[1])).astype(BF16)
    for k in range(count):
        outs[k][0] = plane[k * rows : (k + 1) * rows]


def exchange(cells, own, src, coulomb, table, turn, first_plane, planes):
    count = len(cells)
    rows = cells[0].shape[1]
    nu = coulomb.shape[0]
    area = GY * GZ
    tiles = area // LANES
    macs = planes * area * (2 * own.size + 2 * count * rows * area)

    def whole(array):
        return pl.BlockSpec(array.shape, lambda p: (0,) * array.ndim)

    return pl.pallas_call(
        lambda *refs: exchange_kernel(count, *refs),
        grid=(planes,),
        in_specs=[pl.BlockSpec((tiles, rows, LANES), lambda p: (p, 0, 0))] * count
        + [whole(own), whole(src), pl.BlockSpec((nu, area), lambda p: (0, first_plane + p)), whole(table), whole(turn)],
        out_specs=[pl.BlockSpec((1, rows, area), lambda p: (p, 0, 0))] * count,
        out_shape=[jax.ShapeDtypeStruct((planes, rows, area), BF16)] * count,
        scratch_shapes=[pltpu.VMEM((count * rows, area), BF16)],
        compiler_params=pltpu.CompilerParams(vmem_limit_bytes=VMEM_BYTES),
        cost_estimate=pl.CostEstimate(flops=2 * macs, bytes_accessed=12 * 2**20, transcendentals=0),
        name="exchange_planes",
    )(*cells, own, src, coulomb, table, turn)


def line_kernel(factor, group_rows, count, *refs):
    fields, table_ref, out_ref = refs[1:-2], refs[-2], refs[-1]
    start = pl.multiple_of(pl.program_id(0) * group_rows, group_rows)
    picked = [
        f[p, pl.ds(start, group_rows)]
        for c in range(0, len(fields), count)
        for p in range(fields[c].shape[0])
        for f in fields[c : c + count]
    ]
    lines = dot(table_ref[0], jnp.concatenate(picked, axis=0)) * factor
    lines = lines.astype(BF16)
    for t in range(out_ref.shape[1]):
        tile = lines[:, t * LANES : (t + 1) * LANES]
        out_ref[:, t] = tile.reshape(tile.shape[0] // 2, 2, LANES)


def line_pass(fields, table, device, factor, rows, groups, count):
    area = GY * GZ
    group_rows = rows // groups
    tiles = area // LANES
    height = rows // 2 * GX
    macs = rows * GX * area * table.shape[2]
    spec = pltpu.PrefetchScalarGridSpec(
        num_scalar_prefetch=1,
        grid=(groups,),
        in_specs=[pl.BlockSpec(f.shape, lambda g, d: (0, 0, 0)) for f in fields]
        + [pl.BlockSpec((1,) + table.shape[1:], lambda g, d: (d[0], 0, 0))],
        out_specs=pl.BlockSpec((height // groups, tiles, 2, LANES), lambda g, d: (g, 0, 0, 0)),
    )
    return pl.pallas_call(
        lambda *refs: line_kernel(factor, group_rows, count, *refs),
        grid_spec=spec,
        out_shape=jax.ShapeDtypeStruct((height, tiles, 2, LANES), BF16),
        compiler_params=pltpu.CompilerParams(vmem_limit_bytes=VMEM_BYTES),
        cost_estimate=pl.CostEstimate(flops=2 * macs, bytes_accessed=5 * 2**20, transcendentals=0),
        name="line_pass",
    )(device, *fields, table)


def hop(array, distance, count):
    return lax.ppermute(array, "band", [(i, i ^ distance) for i in range(count)])


def body(orbitals, points, partner, coulomb):
    resident = orbitals[0]
    bands, _, all_cells = resident.shape
    rows = 2 * bands
    count = lax.axis_size("band")
    me = lax.axis_index("band")
    planes = GX // count
    chunks = 2 if planes % 2 == 0 else 1
    chunk_planes = planes // chunks
    plane_tiles = GY * GZ // LANES
    chunk_tiles = chunk_planes * plane_tiles

    order = [0]
    bit = count // 2
    while bit:
        order = order + [k ^ bit for k in order]
        bit //= 2

    tiled = resident.reshape(bands, 2, all_cells // LANES, LANES).transpose(0, 2, 1, 3)

    def block(k, c):
        first = (me ^ k) * (planes * plane_tiles) + c * chunk_tiles
        part = lax.dynamic_slice_in_dim(tiled, first, chunk_tiles, 1)
        return part.transpose(1, 0, 2, 3).reshape(chunk_tiles, rows, LANES)

    received = []
    for c in range(chunks):
        arrivals = {}
        for k in sorted(order, reverse=True):
            arrivals[k] = hop(block(k, c), k, count) if k else block(0, c)
        received.append([arrivals[k] for k in order])

    tiles = tiled.transpose(1, 0, 2, 3).reshape(all_cells // LANES, rows, LANES)
    own_values = pick(tiles, points)
    everyone = lax.all_gather(own_values, "kgrp", axis=0, tiled=False)
    chosen = partner == lax.axis_index("kgrp")
    src_values = jnp.sum(jnp.where(chosen[:, None, None], everyone, jnp.zeros_like(everyone)), axis=0)
    both = jnp.stack([own_values, src_values])[None]
    bit = count // 2
    while bit:
        both = jnp.concatenate([both, hop(both, bit, count)], axis=0)
        bit //= 2

    scale = table_scale(GX)
    turn = jnp.asarray(turn_table(count * rows))
    own_coef, src_coef = coefficients(both, turn)
    plane_t = jnp.asarray(plane_table(scale))
    groups = 2 if bands % 16 == 0 else 1
    line_t = jnp.asarray(line_table(scale, order, planes, bands // groups))

    fields = []
    for c in range(chunks):
        sent = exchange(
            received[c], own_coef, src_coef, coulomb, plane_t, turn, c * chunk_planes, chunk_planes
        )
        back = {}
        for k in sorted(order, reverse=True):
            at = order.index(k)
            back[k] = hop(sent[at], k, count) if k else sent[at]
        fields += [back[k] for k in order]

    factor = 1.0 / (scale * scale * math.sqrt(GX * GY * GZ))
    device = jnp.reshape(me, (1,)).astype(jnp.int32)
    out = line_pass(fields, line_t, device, factor, rows, groups, count)
    out = out.reshape(bands, all_cells // LANES, 2, LANES).transpose(0, 2, 1, 3)
    return out.reshape(1, bands, 2, all_cells)


def solution(mesh):
    return jax.shard_map(
        body,
        mesh=mesh,
        in_specs=(P("kgrp", "band", None, None), P(), P(), P(None, "band")),
        out_specs=P("kgrp", "band", None, None),
        check_vma=False,
    )
```

```python
import math

import jax
import jax.numpy as jnp
import numpy as np
from jax import lax
from jax.experimental import pallas as pl
from jax.experimental.pallas import tpu as pltpu
from jax.sharding import PartitionSpec as P

GX = 32
GY = 32
GZ = 32
LANES = 128
BF16 = jnp.bfloat16
F32 = jnp.float32
VMEM_BYTES = 24 * 1024 * 1024


def round_bf16(values):
    return values.astype(BF16).astype(np.float64)


def table_scale(length):
    cosines = np.cos(2.0 * np.pi * np.arange(length // 4) / length)
    best = (np.inf, 1.0)
    for scale in np.linspace(1.0, 2.0, 8193)[:-1]:
        exact = scale * cosines
        error = float(np.max(np.abs(round_bf16(exact) / exact - 1.0)))
        best = min(best, (error, float(scale)))
    return best[1]


def plane_table(scale):
    cell = np.arange(GY * GZ)
    y, z = cell // GZ, cell % GZ
    turns = (y[:, None] * y[None, :] % GY) / GY + (z[:, None] * z[None, :] % GZ) / GZ
    angle = 2.0 * np.pi * (turns % 1.0)
    return (scale * np.stack([np.cos(angle), np.sin(angle)])).astype(BF16)


def line_table(scale, order, planes, bands):
    count = len(order)
    device = np.arange(count)[:, None, None]
    plane = np.arange(planes)[None, :, None]
    x = planes * (device ^ np.array(order)[None, None, :]) + plane
    kx = np.arange(GX)[None, :, None, None]
    angle = 2.0 * np.pi * (kx * x[:, None] % GX) / GX
    cos_t, sin_t = np.cos(angle), np.sin(angle)
    pair = np.stack([np.stack([cos_t, sin_t], -1), np.stack([-sin_t, cos_t], -1)], 2)
    table = np.zeros((count, bands, GX, 2, planes, count, bands, 2), np.float64)
    for band in range(bands):
        table[:, band, :, :, :, :, band, :] = pair
    return (scale * table).reshape(count, bands * GX * 2, planes * count * bands * 2).astype(BF16)


def turn_table(rows):
    table = np.zeros((rows, rows), np.float32)
    even = np.arange(0, rows, 2)
    table[even, even + 1] = -1.0
    table[even + 1, even] = 1.0
    return table.astype(BF16)


def dot(a, b):
    return jnp.dot(a, b, preferred_element_type=F32)


def pick_kernel(points_ref, tiles_ref, out_ref):
    rows = tiles_ref.shape[1]
    lane = lax.broadcasted_iota(jnp.int32, (rows, LANES), 1)

    @pl.loop(0, out_ref.shape[0])
    def _(group):
        def step(m, total):
            point = points_ref[group * LANES + m]
            tile = tiles_ref[lax.shift_right_logical(point, 7)].astype(F32)
            return jnp.where(lane == m, pltpu.roll(tile, (m - point) & (LANES - 1), 1), total)

        total = lax.fori_loop(0, LANES, step, jnp.zeros((rows, LANES), F32), unroll=32)
        out_ref[group] = total.astype(BF16)


def pick(tiles, points):
    groups = points.shape[0] // LANES
    rows = tiles.shape[1]
    out = pl.pallas_call(
        pick_kernel,
        in_specs=[pl.BlockSpec(memory_space=pltpu.SMEM), pl.BlockSpec(memory_space=pltpu.VMEM)],
        out_specs=pl.BlockSpec(memory_space=pltpu.VMEM),
        out_shape=jax.ShapeDtypeStruct((groups, rows, LANES), BF16),
        compiler_params=pltpu.CompilerParams(vmem_limit_bytes=VMEM_BYTES),
        name="pick_points",
    )(points, tiles)
    return out.transpose(1, 0, 2).reshape(rows, groups * LANES)


def coef_kernel(*refs):
    groups, turn_ref, own_ref, src_ref = refs[:-3], refs[-3], refs[-2], refs[-1]
    nu = groups[0].shape[3]
    own = jnp.concatenate([g[k, 0] for g in groups for k in range(g.shape[0])], axis=0)
    src = jnp.concatenate([g[k, 1] for g in groups for k in range(g.shape[0])], axis=0)
    turn = turn_ref[...]
    own_ref[:nu] = own.astype(F32).T.astype(BF16)
    own_ref[nu:] = dot(turn, own).T.astype(BF16)
    src_ref[:, :nu] = -src
    src_ref[:, nu:] = (-dot(turn, src)).astype(BF16)


def coefficients(groups, turn):
    _, _, rows, nu = groups[0].shape
    high = sum(g.shape[0] for g in groups) * rows
    return pl.pallas_call(
        coef_kernel,
        out_shape=(
            jax.ShapeDtypeStruct((2 * nu, high), BF16),
            jax.ShapeDtypeStruct((high, 2 * nu), BF16),
        ),
        compiler_params=pltpu.CompilerParams(vmem_limit_bytes=VMEM_BYTES),
        cost_estimate=pl.CostEstimate(flops=1, bytes_accessed=1, transcendentals=0),
        name="coefficients",
    )(*groups, turn)


def exchange_kernel(first_plane, planes, cells, pairs, inputs, me_ref, *refs):
    arrays = refs[:inputs]
    own_ref, src_ref, coulomb_ref, table_ref, turn_ref = refs[inputs : inputs + 5]
    outs, after_ref, grid_ref, turned_ref = refs[inputs + 5 : -3], refs[-3], refs[-2], refs[-1]
    me = me_ref[0]
    after_ref[0] = me
    nu = coulomb_ref.shape[0]
    rows = arrays[0].shape[2]
    high = len(cells) * rows
    wide = 2 * LANES
    parts = GY * GZ // wide

    @pl.loop(0, planes)
    def _(p):
        down = pl.ds(pl.multiple_of(p * high, high), high)
        for part in range(parts):
            columns = slice(part * wide, (part + 1) * wide)
            tile = (p * parts + part) * 2
            wave = jnp.concatenate(
                [jnp.concatenate([arrays[a][lead(me), tile + t] for a, lead in cells], axis=0) for t in range(2)],
                axis=1,
            )
            density = dot(own_ref[...], wave)
            here = pl.ds(pl.multiple_of((first_plane + p) * GY * GZ + part * wide, wide), wide)
            coulomb = coulomb_ref[:, here].astype(F32)
            weighted = jnp.concatenate(
                [(coulomb * density[:nu]).astype(BF16), (coulomb * density[nu:]).astype(BF16)], axis=0
            )
            field = dot(src_ref[...], weighted).astype(BF16)
            grid_ref[down, columns] = field
            turned_ref[down, columns] = (-dot(turn_ref[...], field)).astype(BF16)

    waves = (dot(grid_ref[...], table_ref[0]) + dot(turned_ref[...], table_ref[1])).astype(BF16)
    side = me % 2
    for p in range(planes):
        for at, (out, half) in enumerate(pairs):
            block = waves[p * high + at * rows : p * high + (at + 1) * rows]
            if half is None:
                outs[out][p] = block
            else:
                outs[out][side ^ half, p] = block


def exchange(me, cells, own, src, coulomb, table, turn, first_plane, planes, pairs):
    arrays, places = distinct(cells)
    rows = arrays[0].shape[2]
    high = len(cells) * rows
    area = GY * GZ
    outs = 1 + max(out for out, _ in pairs)
    halves = () if pairs[0][1] is None else (2,)
    vmem = pl.BlockSpec(memory_space=pltpu.VMEM)
    smem = pl.BlockSpec(memory_space=pltpu.SMEM)
    *sent, after = pl.pallas_call(
        lambda *refs: exchange_kernel(first_plane, planes, places, pairs, len(arrays), *refs),
        in_specs=[smem] + [vmem] * (len(arrays) + 5),
        out_specs=[vmem] * outs + [smem],
        out_shape=[jax.ShapeDtypeStruct(halves + (planes, rows, area), BF16)] * outs
        + [jax.ShapeDtypeStruct((1,), jnp.int32)],
        scratch_shapes=[pltpu.VMEM((planes * high, area), BF16)] * 2,
        compiler_params=pltpu.CompilerParams(vmem_limit_bytes=VMEM_BYTES),
        cost_estimate=pl.CostEstimate(flops=1, bytes_accessed=1, transcendentals=0),
        name="exchange_planes",
    )(me, *arrays, own, src, coulomb, table, turn)
    return sent, after


def collect_kernel(plan, inputs, me_ref, *refs):
    arrays, outs = refs[:inputs], refs[inputs : inputs + len(plan)]
    buffer, in_sems, out_sems = refs[-3:]
    me = me_ref[0]
    ins, backs = [], []
    for out, picks in enumerate(plan):
        for at, (array, lead) in enumerate(picks):
            n = len(ins)
            ins.append(pltpu.make_async_copy(arrays[array].at[lead(me)], buffer.at[n], in_sems.at[n]))
            backs.append(pltpu.make_async_copy(buffer.at[n], outs[out].at[at], out_sems.at[n]))
    for copy in ins:
        copy.start()
    for copy, back in zip(ins, backs):
        copy.wait()
        back.start()
    for back in backs:
        back.wait()


def distinct(picks):
    arrays, places = [], []
    for array, lead in picks:
        at = next((i for i, a in enumerate(arrays) if a is array), len(arrays))
        if at == len(arrays):
            arrays.append(array)
        places.append((at, lead))
    return arrays, places


def collect(me, wanted):
    arrays, places = distinct([pick for picks in wanted for pick in picks])
    plan, at = [], 0
    for picks in wanted:
        plan.append(places[at : at + len(picks)])
        at += len(picks)
    hbm = pl.BlockSpec(memory_space=pltpu.HBM)
    return pl.pallas_call(
        lambda *refs: collect_kernel(plan, len(arrays), *refs),
        in_specs=[pl.BlockSpec(memory_space=pltpu.SMEM)] + [hbm] * len(arrays),
        out_specs=[hbm] * len(wanted),
        out_shape=[
            jax.ShapeDtypeStruct((len(picks),) + picks[0][0].shape[1:], picks[0][0].dtype) for picks in wanted
        ],
        scratch_shapes=[
            pltpu.VMEM((len(places),) + arrays[0].shape[1:], arrays[0].dtype),
            pltpu.SemaphoreType.DMA((len(places),)),
            pltpu.SemaphoreType.DMA((len(places),)),
        ],
        compiler_params=pltpu.CompilerParams(vmem_limit_bytes=VMEM_BYTES),
        cost_estimate=pl.CostEstimate(flops=1, bytes_accessed=1, transcendentals=0),
        name="collect_blocks",
    )(me, *arrays)


def line_kernel(factor, group_rows, count, *refs):
    fields, table_ref, out_ref = refs[1:-2], refs[-2], refs[-1]
    start = pl.multiple_of(pl.program_id(0) * group_rows, group_rows)
    picked = [
        f[p, pl.ds(start, group_rows)]
        for c in range(0, len(fields), count)
        for p in range(fields[c].shape[0])
        for f in fields[c : c + count]
    ]
    lines = dot(table_ref[0], jnp.concatenate(picked, axis=0)) * factor
    lines = lines.astype(BF16)
    for t in range(out_ref.shape[1]):
        tile = lines[:, t * LANES : (t + 1) * LANES]
        out_ref[:, t] = tile.reshape(tile.shape[0] // 2, 2, LANES)


def line_pass(me, fields, table, factor, rows, groups, count):
    area = GY * GZ
    group_rows = rows // groups
    tiles = area // LANES
    height = rows // 2 * GX

    def picked(array, lead):
        return pl.BlockSpec((None,) + array.shape[1:], lambda g, me: (lead(me[0]), 0, 0, 0))

    spec = pltpu.PrefetchScalarGridSpec(
        num_scalar_prefetch=1,
        grid=(groups,),
        in_specs=[picked(*f) for f in fields]
        + [pl.BlockSpec((1,) + table.shape[1:], lambda g, me: (me[0], 0, 0))],
        out_specs=pl.BlockSpec((height // groups, tiles, 2, LANES), lambda g, me: (g, 0, 0, 0)),
    )
    return pl.pallas_call(
        lambda *refs: line_kernel(factor, group_rows, count, *refs),
        grid_spec=spec,
        out_shape=jax.ShapeDtypeStruct((height, tiles, 2, LANES), BF16),
        compiler_params=pltpu.CompilerParams(vmem_limit_bytes=VMEM_BYTES),
        cost_estimate=pl.CostEstimate(flops=1, bytes_accessed=1, transcendentals=0),
        name="line_pass",
    )(me, *[array for array, _ in fields], table)


def hop(array, distance, count):
    return lax.ppermute(array, "band", [(i, i ^ distance) for i in range(count)])


def body(orbitals, points, partner, coulomb):
    _, bands, _, all_cells = orbitals.shape
    rows = 2 * bands
    count = lax.axis_size("band")
    me = lax.axis_index("band")
    planes = GX // count
    chunks = 2 if planes % 2 == 0 else 1
    chunk_planes = planes // chunks
    plane_tiles = GY * GZ // LANES
    chunk_tiles = chunk_planes * plane_tiles

    order = list(range(0, count, 2)) + list(range(1, count, 2))

    tiles = orbitals.reshape(1, bands, 2, all_cells // LANES, LANES).transpose(0, 3, 1, 2, 4)
    tiles = lax.optimization_barrier(tiles.reshape(all_cells // LANES, rows, LANES))
    blocks = tiles.reshape(count * chunks, chunk_tiles, rows, LANES)
    scale = table_scale(GX)
    turn = jnp.asarray(turn_table(count * rows))
    device = jnp.reshape(me, (1,)).astype(jnp.int32)

    def first(me):
        return 0

    def swap_pairs(pairs, me):
        (other,) = collect(me, [[(pairs[d], lambda me: 1 - me % 2) for d in sorted(pairs)]])
        swapped = hop(other, 1, count)
        return [
            (swapped, lambda me, k=k: k // 2) if k % 2 else (pairs[k], lambda me: me % 2)
            for k in order
        ]

    def cross(c, me):
        wanted = [
            [(blocks, lambda me, d=d, y=y: ((me ^ d) // 2 * 2 + y) * chunks + c) for y in range(2)]
            for d in range(0, count, 2)
        ]
        pairs = dict(zip(range(0, count, 2), collect(me, wanted)))
        return {d: hop(pair, d, count) if d else pair for d, pair in pairs.items()}

    own_values = pick(tiles, points)
    everyone = lax.all_gather(own_values, "kgrp", axis=0, tiled=False)
    chosen = partner == lax.axis_index("kgrp")
    src_values = jnp.sum(jnp.where(chosen[:, None, None], everyone, jnp.zeros_like(everyone)), axis=0)
    both = jnp.stack([own_values, src_values])[None]
    over_z = [both] + [hop(both, d, count) for d in range(2, count, 2)]
    crossing = [cross(c, device) for c in range(chunks)]
    (here,) = collect(device, [[(part, first) for part in over_z]])
    own_coef, src_coef = coefficients([here, hop(here, 1, count)], turn)

    plane_t = jnp.asarray(plane_table(scale))
    groups = 2 if bands % 16 == 0 else 1
    line_t = jnp.asarray(line_table(scale, order, planes, bands // groups))

    received = swap_pairs(crossing[0], device)
    fields = []
    waiting = None
    for c in range(chunks):
        last = c == chunks - 1
        pairs = [(at, None) if last else (k // 2, k % 2) for at, k in enumerate(order)]
        sent, after = exchange(
            device, received, own_coef, src_coef, coulomb, plane_t, turn, c * chunk_planes, chunk_planes, pairs
        )
        if waiting is not None:
            fields += swap_pairs(waiting, after)
        if last:
            back = {}
            for k in sorted(order, reverse=True):
                at = order.index(k)
                back[k] = hop(sent[at], k, count) if k else sent[at]
            fields += [(back[k][None], first) for k in order]
        else:
            waiting = {d: hop(sent[d // 2], d, count) if d else sent[0] for d in range(0, count, 2)}
            received = swap_pairs(crossing[c + 1], after)

    factor = 1.0 / (scale * scale * math.sqrt(GX * GY * GZ))
    out = line_pass(device, fields, line_t, factor, rows, groups, count)
    out = out.reshape(bands, all_cells // LANES, 2, LANES).transpose(0, 2, 1, 3)
    return out.reshape(1, bands, 2, all_cells)


def solution(mesh):
    return jax.shard_map(
        body,
        mesh=mesh,
        in_specs=(P("kgrp", "band", None, None), P(), P(), P(None, "band")),
        out_specs=P("kgrp", "band", None, None),
        check_vma=False,
    )
```

```python
import math

import jax
import jax.numpy as jnp
import numpy as np
from jax import lax
from jax.experimental import pallas as pl
from jax.experimental.pallas import tpu as pltpu
from jax.sharding import PartitionSpec as P

GX = 32
GY = 32
GZ = 32
LANES = 128
BF16 = jnp.bfloat16
F32 = jnp.float32
VMEM_BYTES = 24 * 1024 * 1024
FREE = pl.CostEstimate(flops=1, bytes_accessed=1, transcendentals=0)


def round_bf16(values):
    return values.astype(BF16).astype(np.float64)


def table_scale(length):
    cosines = np.cos(2.0 * np.pi * np.arange(length // 4) / length)
    best = (np.inf, 1.0)
    for scale in np.linspace(1.0, 2.0, 8193)[:-1]:
        exact = scale * cosines
        error = float(np.max(np.abs(round_bf16(exact) / exact - 1.0)))
        best = min(best, (error, float(scale)))
    return best[1]


def plane_table(scale):
    cell = np.arange(GY * GZ)
    y, z = cell // GZ, cell % GZ
    turns = (y[:, None] * y[None, :] % GY) / GY + (z[:, None] * z[None, :] % GZ) / GZ
    angle = 2.0 * np.pi * (turns % 1.0)
    return (scale * np.stack([np.cos(angle), np.sin(angle)])).astype(BF16)


def line_table(scale, order, planes, bands):
    count = len(order)
    device = np.arange(count)[:, None, None]
    plane = np.arange(planes)[None, :, None]
    x = planes * (device ^ np.array(order)[None, None, :]) + plane
    kx = np.arange(GX)[None, :, None, None]
    angle = 2.0 * np.pi * (kx * x[:, None] % GX) / GX
    cos_t, sin_t = np.cos(angle), np.sin(angle)
    pair = np.stack([np.stack([cos_t, sin_t], -1), np.stack([-sin_t, cos_t], -1)], 2)
    table = np.zeros((count, bands, GX, 2, planes, count, bands, 2), np.float64)
    for band in range(bands):
        table[:, band, :, :, :, :, band, :] = pair
    return (scale * table).reshape(count, bands * GX * 2, planes * count * bands * 2).astype(BF16)


def turn_table(rows):
    table = np.zeros((rows, rows), np.float32)
    even = np.arange(0, rows, 2)
    table[even, even + 1] = -1.0
    table[even + 1, even] = 1.0
    return table.astype(BF16)


def dot(a, b):
    return jnp.dot(a, b, preferred_element_type=F32)


def pick_kernel(points_ref, tiles_ref, out_ref):
    rows = tiles_ref.shape[1]
    lane = lax.broadcasted_iota(jnp.int32, (rows, LANES), 1)

    @pl.loop(0, out_ref.shape[0])
    def _(group):
        def step(m, total):
            point = points_ref[group * LANES + m]
            tile = tiles_ref[lax.shift_right_logical(point, 7)].astype(F32)
            return jnp.where(lane == m, pltpu.roll(tile, (m - point) & (LANES - 1), 1), total)

        total = lax.fori_loop(0, LANES, step, jnp.zeros((rows, LANES), F32), unroll=32)
        out_ref[group] = total.astype(BF16)


def pick(tiles, points):
    groups = points.shape[0] // LANES
    rows = tiles.shape[1]
    out = pl.pallas_call(
        pick_kernel,
        in_specs=[pl.BlockSpec(memory_space=pltpu.SMEM), pl.BlockSpec(memory_space=pltpu.VMEM)],
        out_specs=pl.BlockSpec(memory_space=pltpu.VMEM),
        out_shape=jax.ShapeDtypeStruct((groups, rows, LANES), BF16),
        compiler_params=pltpu.CompilerParams(vmem_limit_bytes=VMEM_BYTES),
        name="pick_points",
    )(points, tiles)
    return out


def coef_kernel(picks, inputs, me_ref, *refs):
    arrays, turn_ref, own_ref, src_ref = refs[:inputs], refs[-3], refs[-2], refs[-1]
    values = [arrays[array][lead(me_ref[0])] for array, lead in picks]
    groups = values[0].shape[0] // 2
    nu = groups * LANES
    own = jnp.concatenate([jnp.concatenate([v[g] for g in range(groups)], axis=1) for v in values], axis=0)
    src = jnp.concatenate([jnp.concatenate([v[groups + g] for g in range(groups)], axis=1) for v in values], axis=0)
    turn = turn_ref[...]
    own_ref[:nu] = own.astype(F32).T.astype(BF16)
    own_ref[nu:] = dot(turn, own).T.astype(BF16)
    src_ref[:, :nu] = -src
    src_ref[:, nu:] = (-dot(turn, src)).astype(BF16)


def coefficients(me, values, turn):
    arrays, picks = distinct(values)
    tiles, rows, _ = arrays[0].shape[1:]
    high, nu = len(values) * rows, tiles // 2 * LANES
    return pl.pallas_call(
        lambda *refs: coef_kernel(picks, len(arrays), *refs),
        in_specs=[pl.BlockSpec(memory_space=pltpu.SMEM)] + [pl.BlockSpec(memory_space=pltpu.VMEM)] * (len(arrays) + 1),
        out_shape=(jax.ShapeDtypeStruct((2 * nu, high), BF16), jax.ShapeDtypeStruct((high, 2 * nu), BF16)),
        compiler_params=pltpu.CompilerParams(vmem_limit_bytes=VMEM_BYTES),
        cost_estimate=FREE,
        name="coefficients",
    )(me, *arrays, turn)


def exchange_kernel(first_plane, planes, cells, pairs, inputs, me_ref, *refs):
    arrays = refs[:inputs]
    own_ref, src_ref, coulomb_ref, table_ref, turn_ref = refs[inputs : inputs + 5]
    outs, after_ref, grid_ref, turned_ref = refs[inputs + 5 : -3], refs[-3], refs[-2], refs[-1]
    me = me_ref[0]
    after_ref[0] = me
    nu = coulomb_ref.shape[0]
    rows = arrays[0].shape[2]
    high = len(cells) * rows
    wide = 2 * LANES
    parts = GY * GZ // wide

    @pl.loop(0, planes)
    def _(p):
        down = pl.ds(pl.multiple_of(p * high, high), high)
        for part in range(parts):
            columns = slice(part * wide, (part + 1) * wide)
            tile = (p * parts + part) * 2
            wave = jnp.concatenate(
                [jnp.concatenate([arrays[a][lead(me), tile + t] for a, lead in cells], axis=0) for t in range(2)],
                axis=1,
            )
            density = dot(own_ref[...], wave)
            here = pl.ds(pl.multiple_of((first_plane + p) * GY * GZ + part * wide, wide), wide)
            coulomb = coulomb_ref[:, here].astype(F32)
            weighted = jnp.concatenate(
                [(coulomb * density[:nu]).astype(BF16), (coulomb * density[nu:]).astype(BF16)], axis=0
            )
            field = dot(src_ref[...], weighted).astype(BF16)
            grid_ref[down, columns] = field
            turned_ref[down, columns] = (-dot(turn_ref[...], field)).astype(BF16)

    waves = (dot(grid_ref[...], table_ref[0]) + dot(turned_ref[...], table_ref[1])).astype(BF16)
    side = me % 2
    for p in range(planes):
        for at, (out, half) in enumerate(pairs):
            block = waves[p * high + at * rows : p * high + (at + 1) * rows]
            if half is None:
                outs[out][p] = block
            else:
                outs[out][side ^ half, p] = block


def exchange(me, cells, own, src, coulomb, table, turn, first_plane, planes, pairs):
    arrays, places = distinct(cells)
    rows = arrays[0].shape[2]
    high = len(cells) * rows
    area = GY * GZ
    outs = 1 + max(out for out, _ in pairs)
    halves = () if pairs[0][1] is None else (2,)
    vmem = pl.BlockSpec(memory_space=pltpu.VMEM)
    smem = pl.BlockSpec(memory_space=pltpu.SMEM)
    *sent, after = pl.pallas_call(
        lambda *refs: exchange_kernel(first_plane, planes, places, pairs, len(arrays), *refs),
        in_specs=[smem] + [vmem] * (len(arrays) + 5),
        out_specs=[vmem] * outs + [smem],
        out_shape=[jax.ShapeDtypeStruct(halves + (planes, rows, area), BF16)] * outs
        + [jax.ShapeDtypeStruct((1,), jnp.int32)],
        scratch_shapes=[pltpu.VMEM((planes * high, area), BF16)] * 2,
        compiler_params=pltpu.CompilerParams(vmem_limit_bytes=VMEM_BYTES),
        cost_estimate=FREE,
        name="exchange_planes",
    )(me, *arrays, own, src, coulomb, table, turn)
    return sent, after


def gate_kernel(me_ref, *refs):
    refs[-1][0] = me_ref[0]


def gate(me, arrays):
    smem = pl.BlockSpec(memory_space=pltpu.SMEM)
    return pl.pallas_call(
        gate_kernel,
        in_specs=[smem] + [pl.BlockSpec(memory_space=pl.ANY)] * len(arrays),
        out_specs=smem,
        out_shape=jax.ShapeDtypeStruct((1,), jnp.int32),
        cost_estimate=FREE,
        name="gate",
    )(me, *arrays)


def collect_kernel(plan, inputs, me_ref, *refs):
    arrays, outs = refs[:inputs], refs[inputs : inputs + len(plan)]
    buffer, in_sems, out_sems = refs[-3:]
    me = me_ref[0]
    ins, backs = [], []
    for out, picks in enumerate(plan):
        for at, (array, lead) in enumerate(picks):
            n = len(ins)
            ins.append(pltpu.make_async_copy(arrays[array].at[lead(me)], buffer.at[n], in_sems.at[n]))
            backs.append(pltpu.make_async_copy(buffer.at[n], outs[out].at[at], out_sems.at[n]))
    for copy in ins:
        copy.start()
    for copy, back in zip(ins, backs):
        copy.wait()
        back.start()
    for back in backs:
        back.wait()


def distinct(picks):
    arrays, places = [], []
    for array, lead in picks:
        at = next((i for i, a in enumerate(arrays) if a is array), len(arrays))
        if at == len(arrays):
            arrays.append(array)
        places.append((at, lead))
    return arrays, places


def collect(me, wanted):
    arrays, places = distinct([pick for picks in wanted for pick in picks])
    plan, at = [], 0
    for picks in wanted:
        plan.append(places[at : at + len(picks)])
        at += len(picks)
    hbm = pl.BlockSpec(memory_space=pltpu.HBM)
    return pl.pallas_call(
        lambda *refs: collect_kernel(plan, len(arrays), *refs),
        in_specs=[pl.BlockSpec(memory_space=pltpu.SMEM)] + [pl.BlockSpec(memory_space=pl.ANY)] * len(arrays),
        out_specs=[hbm] * len(wanted),
        out_shape=[
            jax.ShapeDtypeStruct((len(picks),) + picks[0][0].shape[1:], picks[0][0].dtype) for picks in wanted
        ],
        scratch_shapes=[
            pltpu.VMEM((len(places),) + arrays[0].shape[1:], arrays[0].dtype),
            pltpu.SemaphoreType.DMA((len(places),)),
            pltpu.SemaphoreType.DMA((len(places),)),
        ],
        compiler_params=pltpu.CompilerParams(vmem_limit_bytes=VMEM_BYTES),
        cost_estimate=FREE,
        name="collect_blocks",
    )(me, *arrays)


def line_kernel(factor, group_rows, count, *refs):
    fields, table_ref, out_ref = refs[1:-2], refs[-2], refs[-1]
    start = pl.multiple_of(pl.program_id(0) * group_rows, group_rows)
    picked = [
        f[p, pl.ds(start, group_rows)]
        for c in range(0, len(fields), count)
        for p in range(fields[c].shape[0])
        for f in fields[c : c + count]
    ]
    lines = dot(table_ref[0], jnp.concatenate(picked, axis=0)) * factor
    lines = lines.astype(BF16)
    for t in range(out_ref.shape[1]):
        tile = lines[:, t * LANES : (t + 1) * LANES]
        out_ref[:, t] = tile.reshape(tile.shape[0] // 2, 2, LANES)


def line_pass(me, fields, table, factor, rows, groups, count):
    area = GY * GZ
    group_rows = rows // groups
    tiles = area // LANES
    height = rows // 2 * GX

    def picked(array, lead):
        return pl.BlockSpec((None,) + array.shape[1:], lambda g, me: (lead(me[0]), 0, 0, 0))

    spec = pltpu.PrefetchScalarGridSpec(
        num_scalar_prefetch=1,
        grid=(groups,),
        in_specs=[picked(*f) for f in fields]
        + [pl.BlockSpec((1,) + table.shape[1:], lambda g, me: (me[0], 0, 0))],
        out_specs=pl.BlockSpec((height // groups, tiles, 2, LANES), lambda g, me: (g, 0, 0, 0)),
    )
    return pl.pallas_call(
        lambda *refs: line_kernel(factor, group_rows, count, *refs),
        grid_spec=spec,
        out_shape=jax.ShapeDtypeStruct((height, tiles, 2, LANES), BF16),
        compiler_params=pltpu.CompilerParams(vmem_limit_bytes=VMEM_BYTES),
        cost_estimate=FREE,
        name="line_pass",
    )(me, *[array for array, _ in fields], table)


def hop(array, distance, count):
    return lax.ppermute(array, "band", [(i, i ^ distance) for i in range(count)])


def body(orbitals, points, partner, coulomb):
    _, bands, _, all_cells = orbitals.shape
    rows = 2 * bands
    count = lax.axis_size("band")
    me = lax.axis_index("band")
    planes = GX // count
    chunks = 2 if planes % 2 == 0 else 1
    chunk_planes = planes // chunks
    plane_tiles = GY * GZ // LANES
    chunk_tiles = chunk_planes * plane_tiles

    order = list(range(0, count, 2)) + list(range(1, count, 2))

    tiles = orbitals.reshape(1, bands, 2, all_cells // LANES, LANES).transpose(0, 3, 1, 2, 4)
    tiles = lax.optimization_barrier(tiles.reshape(all_cells // LANES, rows, LANES))
    blocks = tiles.reshape(count * chunks, chunk_tiles, rows, LANES)
    scale = table_scale(GX)
    turn = jnp.asarray(turn_table(count * rows))
    device = jnp.reshape(me, (1,)).astype(jnp.int32)

    def first(me):
        return 0

    def swap_pairs(pairs, me):
        (other,) = collect(me, [[(pairs[d], lambda me: 1 - me % 2) for d in sorted(pairs)]])
        swapped = hop(other, 1, count)
        return [
            (swapped, lambda me, k=k: k // 2) if k % 2 else (pairs[k], lambda me: me % 2)
            for k in order
        ]

    def cross(c, distances, me):
        wanted = [
            [(blocks, lambda me, d=d, y=y: ((me ^ d) // 2 * 2 + y) * chunks + c) for y in range(2)]
            for d in distances
        ]
        return {d: hop(pair, d, count) if d else pair for d, pair in zip(distances, collect(me, wanted))}

    def direct(c, distances, me):
        wanted = [[(blocks, lambda me, d=d: (me ^ d) * chunks + c)] for d in distances]
        return {d: hop(block, d, count) for d, block in zip(distances, collect(me, wanted))}

    own_values = pick(tiles, points)
    everyone = lax.all_gather(own_values, "kgrp", axis=0, tiled=False)
    chosen = partner == lax.axis_index("kgrp")
    matched = jnp.sum(jnp.where(chosen[:, None, None, None], everyone, jnp.zeros_like(everyone)), axis=0)
    values = jnp.concatenate([own_values, matched], axis=0)[None]
    over_z = [values] + [hop(values, d, count) for d in range(2, count, 2)]
    (here,) = collect(device, [[(part, first) for part in over_z]])
    there = hop(here, 1, count)
    picks = [(there if k % 2 else here, lambda me, i=k // 2: i) for k in order]
    own_coef, src_coef = coefficients(device, picks, turn)

    received = []
    for c in range(chunks):
        distances = list(range(count // 2, count)) + list(range(1, count // 2))
        arrived = direct(c, distances, gate(device, [values]) if c == 0 else gate(device, [values]))
        received.append([(arrived[k], first) if k else (blocks, lambda me, c=c: me * chunks + c) for k in order])

    plane_t = jnp.asarray(plane_table(scale))
    groups = 2 if bands % 16 == 0 else 1
    line_t = jnp.asarray(line_table(scale, order, planes, bands // groups))

    fields = []
    for c in range(chunks):
        sent, _ = exchange(
            device, received[c], own_coef, src_coef, coulomb, plane_t, turn, c * chunk_planes, chunk_planes,
            [(at, None) for at in range(count)],
        )
        back = {0: sent[0]}
        for k in list(range(count // 2, count)) + list(range(1, count // 2)):
            back[k] = hop(sent[order.index(k)], k, count)
        fields += [(back[k][None], first) for k in order]

    factor = 1.0 / (scale * scale * math.sqrt(GX * GY * GZ))
    out = line_pass(device, fields, line_t, factor, rows, groups, count)
    out = out.reshape(bands, all_cells // LANES, 2, LANES).transpose(0, 2, 1, 3)
    return out.reshape(1, bands, 2, all_cells)


def solution(mesh):
    return jax.shard_map(
        body,
        mesh=mesh,
        in_specs=(P("kgrp", "band", None, None), P(), P(), P(None, "band")),
        out_specs=P("kgrp", "band", None, None),
        check_vma=False,
    )
```

```python
import math

import jax
import jax.numpy as jnp
import numpy as np
from jax import lax
from jax.experimental import pallas as pl
from jax.experimental.pallas import tpu as pltpu
from jax.sharding import PartitionSpec as P

GX = 32
GY = 32
GZ = 32
LANES = 128
BF16 = jnp.bfloat16
F32 = jnp.float32
VMEM_BYTES = 24 * 1024 * 1024
FREE = pl.CostEstimate(flops=1, bytes_accessed=1, transcendentals=0)


def round_bf16(values):
    return values.astype(BF16).astype(np.float64)


def table_scale(length):
    cosines = np.cos(2.0 * np.pi * np.arange(length // 4) / length)
    best = (np.inf, 1.0)
    for scale in np.linspace(1.0, 2.0, 8193)[:-1]:
        exact = scale * cosines
        error = float(np.max(np.abs(round_bf16(exact) / exact - 1.0)))
        best = min(best, (error, float(scale)))
    return best[1]


def plane_table(scale):
    cell = np.arange(GY * GZ)
    y, z = cell // GZ, cell % GZ
    turns = (y[:, None] * y[None, :] % GY) / GY + (z[:, None] * z[None, :] % GZ) / GZ
    angle = 2.0 * np.pi * (turns % 1.0)
    return (scale * np.stack([np.cos(angle), np.sin(angle)])).astype(BF16)


def line_table(scale, order, planes, bands):
    count = len(order)
    device = np.arange(count)[:, None, None]
    plane = np.arange(planes)[None, :, None]
    x = planes * (device ^ np.array(order)[None, None, :]) + plane
    kx = np.arange(GX)[None, :, None, None]
    angle = 2.0 * np.pi * (kx * x[:, None] % GX) / GX
    cos_t, sin_t = np.cos(angle), np.sin(angle)
    pair = np.stack([np.stack([cos_t, sin_t], -1), np.stack([-sin_t, cos_t], -1)], 2)
    table = np.zeros((count, bands, GX, 2, planes, count, bands, 2), np.float64)
    for band in range(bands):
        table[:, band, :, :, :, :, band, :] = pair
    return (scale * table).reshape(count, bands * GX * 2, planes * count * bands * 2).astype(BF16)


def turn_table(rows):
    table = np.zeros((rows, rows), np.float32)
    even = np.arange(0, rows, 2)
    table[even, even + 1] = -1.0
    table[even + 1, even] = 1.0
    return table.astype(BF16)


def dot(a, b):
    return jnp.dot(a, b, preferred_element_type=F32)


def pick_kernel(points_ref, tiles_ref, *refs):
    out_ref = refs[-1]
    rows = tiles_ref.shape[1]
    lane = lax.broadcasted_iota(jnp.int32, (rows, LANES), 1)

    @pl.loop(0, out_ref.shape[0])
    def _(group):
        def step(m, total):
            point = points_ref[group * LANES + m]
            tile = tiles_ref[lax.shift_right_logical(point, 7)].astype(F32)
            return jnp.where(lane == m, pltpu.roll(tile, (m - point) & (LANES - 1), 1), total)

        total = lax.fori_loop(0, LANES, step, jnp.zeros((rows, LANES), F32), unroll=32)
        out_ref[group] = total.astype(BF16)


def pick(tiles, points, ahead):
    groups = points.shape[0] // LANES
    rows = tiles.shape[1]
    out = pl.pallas_call(
        pick_kernel,
        in_specs=[pl.BlockSpec(memory_space=pltpu.SMEM), pl.BlockSpec(memory_space=pltpu.VMEM)]
        + [pl.BlockSpec(memory_space=pl.ANY)] * len(ahead),
        out_specs=pl.BlockSpec(memory_space=pltpu.VMEM),
        out_shape=jax.ShapeDtypeStruct((groups, rows, LANES), BF16),
        compiler_params=pltpu.CompilerParams(vmem_limit_bytes=VMEM_BYTES),
        name="pick_points",
    )(points, tiles, *ahead)
    return out


def coef_kernel(picks, inputs, me_ref, *refs):
    arrays, turn_ref, own_ref, src_ref = refs[:inputs], refs[inputs], refs[-2], refs[-1]
    values = [arrays[array][lead(me_ref[0])] for array, lead in picks]
    groups = values[0].shape[0] // 2
    nu = groups * LANES
    own = jnp.concatenate([jnp.concatenate([v[g] for g in range(groups)], axis=1) for v in values], axis=0)
    src = jnp.concatenate([jnp.concatenate([v[groups + g] for g in range(groups)], axis=1) for v in values], axis=0)
    turn = turn_ref[...]
    own_ref[:nu] = own.astype(F32).T.astype(BF16)
    own_ref[nu:] = dot(turn, own).T.astype(BF16)
    src_ref[:, :nu] = -src
    src_ref[:, nu:] = (-dot(turn, src)).astype(BF16)


def coefficients(me, values, turn, held):
    arrays, picks = distinct(values)
    tiles, rows, _ = arrays[0].shape[1:]
    high, nu = len(values) * rows, tiles // 2 * LANES
    return pl.pallas_call(
        lambda *refs: coef_kernel(picks, len(arrays), *refs),
        in_specs=[pl.BlockSpec(memory_space=pltpu.SMEM)] + [pl.BlockSpec(memory_space=pltpu.VMEM)] * (len(arrays) + 1 + len(held)),
        out_shape=(jax.ShapeDtypeStruct((2 * nu, high), BF16), jax.ShapeDtypeStruct((high, 2 * nu), BF16)),
        compiler_params=pltpu.CompilerParams(vmem_limit_bytes=VMEM_BYTES),
        cost_estimate=FREE,
        name="coefficients",
    )(me, *arrays, turn, *held)


def exchange_kernel(first_plane, planes, cells, pairs, inputs, me_ref, *refs):
    arrays = refs[:inputs]
    own_ref, src_ref, coulomb_ref, table_ref, turn_ref = refs[inputs : inputs + 5]
    outs, after_ref, grid_ref, turned_ref = refs[inputs + 5 : -3], refs[-3], refs[-2], refs[-1]
    me = me_ref[0]
    after_ref[0] = me
    nu = coulomb_ref.shape[0]
    rows = arrays[0].shape[2]
    high = len(cells) * rows
    wide = 2 * LANES
    parts = GY * GZ // wide

    @pl.loop(0, planes)
    def _(p):
        down = pl.ds(pl.multiple_of(p * high, high), high)
        for part in range(parts):
            columns = slice(part * wide, (part + 1) * wide)
            tile = (p * parts + part) * 2
            wave = jnp.concatenate(
                [jnp.concatenate([arrays[a][lead(me), tile + t] for a, lead in cells], axis=0) for t in range(2)],
                axis=1,
            )
            density = dot(own_ref[...], wave)
            here = pl.ds(pl.multiple_of((first_plane + p) * GY * GZ + part * wide, wide), wide)
            coulomb = coulomb_ref[:, here].astype(F32)
            weighted = jnp.concatenate(
                [(coulomb * density[:nu]).astype(BF16), (coulomb * density[nu:]).astype(BF16)], axis=0
            )
            field = dot(src_ref[...], weighted).astype(BF16)
            grid_ref[down, columns] = field
            turned_ref[down, columns] = (-dot(turn_ref[...], field)).astype(BF16)

    waves = (dot(grid_ref[...], table_ref[0]) + dot(turned_ref[...], table_ref[1])).astype(BF16)
    side = me % 2
    for p in range(planes):
        for at, (out, half) in enumerate(pairs):
            block = waves[p * high + at * rows : p * high + (at + 1) * rows]
            if half is None:
                outs[out][p] = block
            else:
                outs[out][side ^ half, p] = block


def exchange(me, cells, own, src, coulomb, table, turn, first_plane, planes, pairs):
    arrays, places = distinct(cells)
    rows = arrays[0].shape[2]
    high = len(cells) * rows
    area = GY * GZ
    outs = 1 + max(out for out, _ in pairs)
    halves = () if pairs[0][1] is None else (2,)
    vmem = pl.BlockSpec(memory_space=pltpu.VMEM)
    smem = pl.BlockSpec(memory_space=pltpu.SMEM)
    *sent, after = pl.pallas_call(
        lambda *refs: exchange_kernel(first_plane, planes, places, pairs, len(arrays), *refs),
        in_specs=[smem] + [vmem] * (len(arrays) + 5),
        out_specs=[vmem] * outs + [smem],
        out_shape=[jax.ShapeDtypeStruct(halves + (planes, rows, area), BF16)] * outs
        + [jax.ShapeDtypeStruct((1,), jnp.int32)],
        scratch_shapes=[pltpu.VMEM((planes * high, area), BF16)] * 2,
        compiler_params=pltpu.CompilerParams(vmem_limit_bytes=VMEM_BYTES),
        cost_estimate=FREE,
        name="exchange_planes",
    )(me, *arrays, own, src, coulomb, table, turn)
    return sent, after


def collect_kernel(plan, inputs, me_ref, *refs):
    arrays, outs = refs[:inputs], refs[inputs : inputs + len(plan)]
    buffer, in_sems, out_sems = refs[-3:]
    me = me_ref[0]
    ins, backs = [], []
    for out, picks in enumerate(plan):
        for at, (array, lead) in enumerate(picks):
            n = len(ins)
            ins.append(pltpu.make_async_copy(arrays[array].at[lead(me)], buffer.at[n], in_sems.at[n]))
            backs.append(pltpu.make_async_copy(buffer.at[n], outs[out].at[at], out_sems.at[n]))
    for copy in ins:
        copy.start()
    for copy, back in zip(ins, backs):
        copy.wait()
        back.start()
    for back in backs:
        back.wait()


def distinct(picks):
    arrays, places = [], []
    for array, lead in picks:
        at = next((i for i, a in enumerate(arrays) if a is array), len(arrays))
        if at == len(arrays):
            arrays.append(array)
        places.append((at, lead))
    return arrays, places


def send_kernel(leads, me_ref, blocks_ref, *refs):
    outs, sems = refs[:-1], refs[-1]
    copies = [
        pltpu.make_async_copy(blocks_ref.at[lead(me_ref[0])], out.at[0], sems.at[n])
        for n, (lead, out) in enumerate(zip(leads, outs))
    ]
    for copy in copies:
        copy.start()
    for copy in copies:
        copy.wait()


def send_blocks(me, blocks, leads):
    return pl.pallas_call(
        lambda *refs: send_kernel(leads, *refs),
        in_specs=[pl.BlockSpec(memory_space=pltpu.SMEM), pl.BlockSpec(memory_space=pltpu.VMEM)],
        out_specs=[pl.BlockSpec(memory_space=pltpu.HBM)] * len(leads),
        out_shape=[jax.ShapeDtypeStruct((1,) + blocks.shape[1:], blocks.dtype)] * len(leads),
        scratch_shapes=[pltpu.SemaphoreType.DMA((len(leads),))],
        compiler_params=pltpu.CompilerParams(vmem_limit_bytes=VMEM_BYTES),
        cost_estimate=FREE,
        name="send_blocks",
    )(me, blocks)


def collect(me, wanted):
    arrays, places = distinct([pick for picks in wanted for pick in picks])
    plan, at = [], 0
    for picks in wanted:
        plan.append(places[at : at + len(picks)])
        at += len(picks)
    hbm = pl.BlockSpec(memory_space=pltpu.HBM)
    return pl.pallas_call(
        lambda *refs: collect_kernel(plan, len(arrays), *refs),
        in_specs=[pl.BlockSpec(memory_space=pltpu.SMEM)] + [pl.BlockSpec(memory_space=pl.ANY)] * len(arrays),
        out_specs=[hbm] * len(wanted),
        out_shape=[
            jax.ShapeDtypeStruct((len(picks),) + picks[0][0].shape[1:], picks[0][0].dtype) for picks in wanted
        ],
        scratch_shapes=[
            pltpu.VMEM((len(places),) + arrays[0].shape[1:], arrays[0].dtype),
            pltpu.SemaphoreType.DMA((len(places),)),
            pltpu.SemaphoreType.DMA((len(places),)),
        ],
        compiler_params=pltpu.CompilerParams(vmem_limit_bytes=VMEM_BYTES),
        cost_estimate=FREE,
        name="collect_blocks",
    )(me, *arrays)


def line_kernel(factor, group_rows, count, *refs):
    fields, table_ref, out_ref = refs[1:-2], refs[-2], refs[-1]
    start = pl.multiple_of(pl.program_id(0) * group_rows, group_rows)
    picked = [
        f[p, pl.ds(start, group_rows)]
        for c in range(0, len(fields), count)
        for p in range(fields[c].shape[0])
        for f in fields[c : c + count]
    ]
    lines = dot(table_ref[0], jnp.concatenate(picked, axis=0)) * factor
    lines = lines.astype(BF16)
    for t in range(out_ref.shape[1]):
        tile = lines[:, t * LANES : (t + 1) * LANES]
        out_ref[:, t] = tile.reshape(tile.shape[0] // 2, 2, LANES)


def line_pass(me, fields, table, factor, rows, groups, count):
    area = GY * GZ
    group_rows = rows // groups
    tiles = area // LANES
    height = rows // 2 * GX

    def picked(array, lead):
        return pl.BlockSpec((None,) + array.shape[1:], lambda g, me: (lead(me[0]), 0, 0, 0))

    spec = pltpu.PrefetchScalarGridSpec(
        num_scalar_prefetch=1,
        grid=(groups,),
        in_specs=[picked(*f) for f in fields]
        + [pl.BlockSpec((1,) + table.shape[1:], lambda g, me: (me[0], 0, 0))],
        out_specs=pl.BlockSpec((height // groups, tiles, 2, LANES), lambda g, me: (g, 0, 0, 0)),
    )
    return pl.pallas_call(
        lambda *refs: line_kernel(factor, group_rows, count, *refs),
        grid_spec=spec,
        out_shape=jax.ShapeDtypeStruct((height, tiles, 2, LANES), BF16),
        compiler_params=pltpu.CompilerParams(vmem_limit_bytes=VMEM_BYTES),
        cost_estimate=FREE,
        name="line_pass",
    )(me, *[array for array, _ in fields], table)


def hop(array, distance, count):
    return lax.ppermute(array, "band", [(i, i ^ distance) for i in range(count)])


def body(orbitals, points, partner, coulomb):
    _, bands, _, all_cells = orbitals.shape
    rows = 2 * bands
    count = lax.axis_size("band")
    me = lax.axis_index("band")
    planes = GX // count
    chunks = 2 if planes % 2 == 0 else 1
    chunk_planes = planes // chunks
    plane_tiles = GY * GZ // LANES
    chunk_tiles = chunk_planes * plane_tiles

    order = list(range(0, count, 2)) + list(range(1, count, 2))
    far = count // 2
    order_back = [0, 2] + list(range(far, count)) + [k for k in range(far - 1, 0, -1) if k != 2]

    tiles = orbitals.reshape(1, bands, 2, all_cells // LANES, LANES).transpose(0, 3, 1, 2, 4)
    tiles = lax.optimization_barrier(tiles.reshape(all_cells // LANES, rows, LANES))
    blocks = tiles.reshape(count * chunks, chunk_tiles, rows, LANES)
    scale = table_scale(GX)
    turn = jnp.asarray(turn_table(count * rows))
    device = jnp.reshape(me, (1,)).astype(jnp.int32)

    def first(me):
        return 0

    def blocks_for(c, distances, me):
        return send_blocks(me, blocks, [lambda me, d=d: (me ^ d) * chunks + c for d in distances])

    distances = list(range(count // 2, count)) + list(range(1, count // 2))
    late = distances[len(distances) - 1 :]
    sends = [blocks_for(c, [d for d in distances if c == 0 or d not in late], device) for c in range(chunks)]
    own_values = pick(tiles, points, sends[0])
    everyone = lax.all_gather(own_values, "kgrp", axis=0, tiled=False)
    chosen = partner == lax.axis_index("kgrp")
    matched = jnp.sum(jnp.where(chosen[:, None, None, None], everyone, jnp.zeros_like(everyone)), axis=0)
    values = jnp.concatenate([own_values, matched], axis=0)[None]
    over_z = [values] + [hop(values, d, count) for d in range(2, count, 2)]
    (here,) = collect(device, [[(part, first) for part in over_z]])
    there = hop(here, 1, count)
    plane_t = jnp.asarray(plane_table(scale))
    picks = [(there if k % 2 else here, lambda me, i=k // 2: i) for k in order]
    own_coef, src_coef = coefficients(device, picks, turn, [coulomb, plane_t])

    received = []
    for c in range(chunks):
        distances = list(range(count // 2, count)) + list(range(1, count // 2))
        arrived = {
            d: hop(block, d, count)
            for d, block in zip([d for d in distances if c == 0 or d not in late], sends[c])
        }
        received.append(arrived)

    groups = 2 if bands % 16 == 0 else 1
    line_t = jnp.asarray(line_table(scale, order_back, planes, bands // groups))

    fields = []
    for c in range(chunks):
        arrived = received[c]
        if c:
            arrived.update({d: hop(block, d, count) for d, block in zip(late, blocks_for(c, late, after))})
        here = [(arrived[k], first) if k else (blocks, lambda me, c=c: me * chunks + c) for k in order]
        sent, after = exchange(
            device, here, own_coef, src_coef, coulomb, plane_t, turn, c * chunk_planes, chunk_planes,
            [(at, None) for at in range(count)],
        )
        back = {0: sent[0]}
        for k in list(range(count // 2, count)) + list(range(1, count // 2)):
            back[k] = hop(sent[order.index(k)], k, count)
        fields += [(back[k][None], first) for k in order_back]

    factor = 1.0 / (scale * scale * math.sqrt(GX * GY * GZ))
    out = line_pass(device, fields, line_t, factor, rows, groups, count)
    out = out.reshape(bands, all_cells // LANES, 2, LANES).transpose(0, 2, 1, 3)
    return out.reshape(1, bands, 2, all_cells)


def solution(mesh):
    return jax.shard_map(
        body,
        mesh=mesh,
        in_specs=(P("kgrp", "band", None, None), P(), P(), P(None, "band")),
        out_specs=P("kgrp", "band", None, None),
        check_vma=False,
    )
```

```python
import math

import jax
import jax.numpy as jnp
import numpy as np
from jax import lax
from jax.experimental import pallas as pl
from jax.experimental.pallas import tpu as pltpu
from jax.sharding import PartitionSpec as P

GX = 32
GY = 32
GZ = 32
LANES = 128
BF16 = jnp.bfloat16
F32 = jnp.float32
VMEM_BYTES = 24 * 1024 * 1024
FREE = pl.CostEstimate(flops=1, bytes_accessed=1, transcendentals=0)


def round_bf16(values):
    return values.astype(BF16).astype(np.float64)


def table_scale(length):
    cosines = np.cos(2.0 * np.pi * np.arange(length // 4) / length)
    best = (np.inf, 1.0)
    for scale in np.linspace(1.0, 2.0, 8193)[:-1]:
        exact = scale * cosines
        error = float(np.max(np.abs(round_bf16(exact) / exact - 1.0)))
        best = min(best, (error, float(scale)))
    return best[1]


def plane_table(scale):
    cell = np.arange(GY * GZ)
    y, z = cell // GZ, cell % GZ
    turns = (y[:, None] * y[None, :] % GY) / GY + (z[:, None] * z[None, :] % GZ) / GZ
    angle = 2.0 * np.pi * (turns % 1.0)
    return (scale * np.stack([np.cos(angle), np.sin(angle)])).astype(BF16)


def line_table(scale, order, planes, bands):
    count = len(order)
    device = np.arange(count)[:, None, None]
    plane = np.arange(planes)[None, :, None]
    x = planes * (device ^ np.array(order)[None, None, :]) + plane
    kx = np.arange(GX)[None, :, None, None]
    angle = 2.0 * np.pi * (kx * x[:, None] % GX) / GX
    cos_t, sin_t = np.cos(angle), np.sin(angle)
    pair = np.stack([np.stack([cos_t, sin_t], -1), np.stack([-sin_t, cos_t], -1)], 2)
    table = np.zeros((count, bands, GX, 2, planes, count, bands, 2), np.float64)
    for band in range(bands):
        table[:, band, :, :, :, :, band, :] = pair
    return (scale * table).reshape(count, bands * GX * 2, planes * count * bands * 2).astype(BF16)


def turn_table(rows):
    table = np.zeros((rows, rows), np.float32)
    even = np.arange(0, rows, 2)
    table[even, even + 1] = -1.0
    table[even + 1, even] = 1.0
    return table.astype(BF16)


def dot(a, b):
    return jnp.dot(a, b, preferred_element_type=F32)


def pick_kernel(points_ref, tiles_ref, *refs):
    out_ref = refs[-1]
    rows = tiles_ref.shape[1]
    lane = lax.broadcasted_iota(jnp.int32, (rows, LANES), 1)

    @pl.loop(0, out_ref.shape[0])
    def _(group):
        def step(m, total):
            point = points_ref[group * LANES + m]
            tile = tiles_ref[lax.shift_right_logical(point, 7)].astype(F32)
            return jnp.where(lane == m, pltpu.roll(tile, (m - point) & (LANES - 1), 1), total)

        total = lax.fori_loop(0, LANES, step, jnp.zeros((rows, LANES), F32), unroll=128)
        out_ref[group] = total.astype(BF16)


def pick(tiles, points, ahead):
    groups = points.shape[0] // LANES
    rows = tiles.shape[1]
    out = pl.pallas_call(
        pick_kernel,
        in_specs=[pl.BlockSpec(memory_space=pltpu.SMEM), pl.BlockSpec(memory_space=pltpu.VMEM)]
        + [pl.BlockSpec(memory_space=pl.ANY)] * len(ahead),
        out_specs=pl.BlockSpec(memory_space=pltpu.VMEM),
        out_shape=jax.ShapeDtypeStruct((groups, rows, LANES), BF16),
        compiler_params=pltpu.CompilerParams(vmem_limit_bytes=VMEM_BYTES),
        name="pick_points",
    )(points, tiles, *ahead)
    return out


def coef_kernel(picks, inputs, me_ref, *refs):
    arrays, turn_ref, own_ref, src_ref = refs[:inputs], refs[inputs], refs[-2], refs[-1]
    values = [arrays[array][lead(me_ref[0])] for array, lead in picks]
    groups = values[0].shape[0] // 2
    nu = groups * LANES
    own = jnp.concatenate([jnp.concatenate([v[g] for g in range(groups)], axis=1) for v in values], axis=0)
    src = jnp.concatenate([jnp.concatenate([v[groups + g] for g in range(groups)], axis=1) for v in values], axis=0)
    turn = turn_ref[...]
    own_ref[:nu] = own.astype(F32).T.astype(BF16)
    own_ref[nu:] = dot(turn, own).T.astype(BF16)
    src_ref[:, :nu] = -src
    src_ref[:, nu:] = (-dot(turn, src)).astype(BF16)


def coefficients(me, values, turn, held):
    arrays, picks = distinct(values)
    tiles, rows, _ = arrays[0].shape[1:]
    high, nu = len(values) * rows, tiles // 2 * LANES
    return pl.pallas_call(
        lambda *refs: coef_kernel(picks, len(arrays), *refs),
        in_specs=[pl.BlockSpec(memory_space=pltpu.SMEM)] + [pl.BlockSpec(memory_space=pltpu.VMEM)] * (len(arrays) + 1 + len(held)),
        out_shape=(jax.ShapeDtypeStruct((2 * nu, high), BF16), jax.ShapeDtypeStruct((high, 2 * nu), BF16)),
        compiler_params=pltpu.CompilerParams(vmem_limit_bytes=VMEM_BYTES),
        cost_estimate=FREE,
        name="coefficients",
    )(me, *arrays, turn, *held)


def exchange_kernel(first_plane, planes, cells, pairs, inputs, me_ref, *refs):
    arrays = refs[:inputs]
    own_ref, src_ref, coulomb_ref, table_ref, turn_ref = refs[inputs : inputs + 5]
    outs, after_ref, grid_ref, turned_ref = refs[inputs + 5 : -3], refs[-3], refs[-2], refs[-1]
    me = me_ref[0]
    after_ref[0] = me
    nu = coulomb_ref.shape[0]
    rows = arrays[0].shape[2]
    high = len(cells) * rows
    wide = 2 * LANES
    parts = GY * GZ // wide

    @pl.loop(0, planes)
    def _(p):
        down = pl.ds(pl.multiple_of(p * high, high), high)
        for part in range(parts):
            columns = slice(part * wide, (part + 1) * wide)
            tile = (p * parts + part) * 2
            wave = jnp.concatenate(
                [jnp.concatenate([arrays[a][lead(me), tile + t] for a, lead in cells], axis=0) for t in range(2)],
                axis=1,
            )
            density = dot(own_ref[...], wave)
            here = pl.ds(pl.multiple_of((first_plane + p) * GY * GZ + part * wide, wide), wide)
            coulomb = coulomb_ref[:, here].astype(F32)
            weighted = jnp.concatenate(
                [(coulomb * density[:nu]).astype(BF16), (coulomb * density[nu:]).astype(BF16)], axis=0
            )
            field = dot(src_ref[...], weighted).astype(BF16)
            grid_ref[down, columns] = field
            turned_ref[down, columns] = (-dot(turn_ref[...], field)).astype(BF16)

    waves = (dot(grid_ref[...], table_ref[0]) + dot(turned_ref[...], table_ref[1])).astype(BF16)
    side = me % 2
    for p in range(planes):
        for at, (out, half) in enumerate(pairs):
            block = waves[p * high + at * rows : p * high + (at + 1) * rows]
            if half is None:
                outs[out][p] = block
            else:
                outs[out][side ^ half, p] = block


def exchange(me, cells, own, src, coulomb, table, turn, first_plane, planes, pairs):
    arrays, places = distinct(cells)
    rows = arrays[0].shape[2]
    high = len(cells) * rows
    area = GY * GZ
    outs = 1 + max(out for out, _ in pairs)
    halves = () if pairs[0][1] is None else (2,)
    vmem = pl.BlockSpec(memory_space=pltpu.VMEM)
    smem = pl.BlockSpec(memory_space=pltpu.SMEM)
    *sent, after = pl.pallas_call(
        lambda *refs: exchange_kernel(first_plane, planes, places, pairs, len(arrays), *refs),
        in_specs=[smem] + [vmem] * (len(arrays) + 5),
        out_specs=[vmem] * outs + [smem],
        out_shape=[jax.ShapeDtypeStruct(halves + (planes, rows, area), BF16)] * outs
        + [jax.ShapeDtypeStruct((1,), jnp.int32)],
        scratch_shapes=[pltpu.VMEM((planes * high, area), BF16)] * 2,
        compiler_params=pltpu.CompilerParams(vmem_limit_bytes=VMEM_BYTES),
        cost_estimate=FREE,
        name="exchange_planes",
    )(me, *arrays, own, src, coulomb, table, turn)
    return sent, after


def collect_kernel(plan, inputs, me_ref, *refs):
    arrays, outs = refs[:inputs], refs[inputs : inputs + len(plan)]
    buffer, in_sems, out_sems = refs[-3:]
    me = me_ref[0]
    ins, backs = [], []
    for out, picks in enumerate(plan):
        for at, (array, lead) in enumerate(picks):
            n = len(ins)
            ins.append(pltpu.make_async_copy(arrays[array].at[lead(me)], buffer.at[n], in_sems.at[n]))
            backs.append(pltpu.make_async_copy(buffer.at[n], outs[out].at[at], out_sems.at[n]))
    for copy in ins:
        copy.start()
    for copy, back in zip(ins, backs):
        copy.wait()
        back.start()
    for back in backs:
        back.wait()


def distinct(picks):
    arrays, places = [], []
    for array, lead in picks:
        at = next((i for i, a in enumerate(arrays) if a is array), len(arrays))
        if at == len(arrays):
            arrays.append(array)
        places.append((at, lead))
    return arrays, places


def send_kernel(leads, me_ref, blocks_ref, *refs):
    outs, sems = refs[:-1], refs[-1]
    copies = [
        pltpu.make_async_copy(blocks_ref.at[lead(me_ref[0])], out.at[0], sems.at[n])
        for n, (lead, out) in enumerate(zip(leads, outs))
    ]
    for copy in copies:
        copy.start()
    for copy in copies:
        copy.wait()


def send_blocks(me, blocks, leads):
    return pl.pallas_call(
        lambda *refs: send_kernel(leads, *refs),
        in_specs=[pl.BlockSpec(memory_space=pltpu.SMEM), pl.BlockSpec(memory_space=pltpu.VMEM)],
        out_specs=[pl.BlockSpec(memory_space=pltpu.HBM)] * len(leads),
        out_shape=[jax.ShapeDtypeStruct((1,) + blocks.shape[1:], blocks.dtype)] * len(leads),
        scratch_shapes=[pltpu.SemaphoreType.DMA((len(leads),))],
        compiler_params=pltpu.CompilerParams(vmem_limit_bytes=VMEM_BYTES),
        cost_estimate=FREE,
        name="send_blocks",
    )(me, blocks)


def collect(me, wanted):
    arrays, places = distinct([pick for picks in wanted for pick in picks])
    plan, at = [], 0
    for picks in wanted:
        plan.append(places[at : at + len(picks)])
        at += len(picks)
    hbm = pl.BlockSpec(memory_space=pltpu.HBM)
    return pl.pallas_call(
        lambda *refs: collect_kernel(plan, len(arrays), *refs),
        in_specs=[pl.BlockSpec(memory_space=pltpu.SMEM)] + [pl.BlockSpec(memory_space=pl.ANY)] * len(arrays),
        out_specs=[hbm] * len(wanted),
        out_shape=[
            jax.ShapeDtypeStruct((len(picks),) + picks[0][0].shape[1:], picks[0][0].dtype) for picks in wanted
        ],
        scratch_shapes=[
            pltpu.VMEM((len(places),) + arrays[0].shape[1:], arrays[0].dtype),
            pltpu.SemaphoreType.DMA((len(places),)),
            pltpu.SemaphoreType.DMA((len(places),)),
        ],
        compiler_params=pltpu.CompilerParams(vmem_limit_bytes=VMEM_BYTES),
        cost_estimate=FREE,
        name="collect_blocks",
    )(me, *arrays)


def line_kernel(factor, group_rows, count, *refs):
    fields, table_ref, out_ref = refs[1:-2], refs[-2], refs[-1]
    start = pl.multiple_of(pl.program_id(0) * group_rows, group_rows)
    picked = [
        f[p, pl.ds(start, group_rows)]
        for c in range(0, len(fields), count)
        for p in range(fields[c].shape[0])
        for f in fields[c : c + count]
    ]
    lines = dot(table_ref[0], jnp.concatenate(picked, axis=0)) * factor
    lines = lines.astype(BF16)
    for t in range(out_ref.shape[1]):
        tile = lines[:, t * LANES : (t + 1) * LANES]
        out_ref[:, t] = tile.reshape(tile.shape[0] // 2, 2, LANES)


def line_pass(me, fields, table, factor, rows, groups, count):
    area = GY * GZ
    group_rows = rows // groups
    tiles = area // LANES
    height = rows // 2 * GX

    def picked(array, lead):
        return pl.BlockSpec((None,) + array.shape[1:], lambda g, me: (lead(me[0]), 0, 0, 0))

    spec = pltpu.PrefetchScalarGridSpec(
        num_scalar_prefetch=1,
        grid=(groups,),
        in_specs=[picked(*f) for f in fields]
        + [pl.BlockSpec((1,) + table.shape[1:], lambda g, me: (me[0], 0, 0))],
        out_specs=pl.BlockSpec((height // groups, tiles, 2, LANES), lambda g, me: (g, 0, 0, 0)),
    )
    return pl.pallas_call(
        lambda *refs: line_kernel(factor, group_rows, count, *refs),
        grid_spec=spec,
        out_shape=jax.ShapeDtypeStruct((height, tiles, 2, LANES), BF16),
        compiler_params=pltpu.CompilerParams(vmem_limit_bytes=VMEM_BYTES),
        cost_estimate=FREE,
        name="line_pass",
    )(me, *[array for array, _ in fields], table)


def hop(array, distance, count):
    return lax.ppermute(array, "band", [(i, i ^ distance) for i in range(count)])


def body(orbitals, points, partner, coulomb):
    _, bands, _, all_cells = orbitals.shape
    rows = 2 * bands
    count = lax.axis_size("band")
    me = lax.axis_index("band")
    planes = GX // count
    chunks = 2 if planes % 2 == 0 else 1
    chunk_planes = planes // chunks
    plane_tiles = GY * GZ // LANES
    chunk_tiles = chunk_planes * plane_tiles

    far = count // 2
    order = list(dict.fromkeys(k for k in [0, far, 2, 1, far + 1, far + 2, *range(count)] if k < count))
    order_back = list(dict.fromkeys(k for k in [0, 2, *range(far, count), *range(far - 1, 0, -1)] if k < count))

    tiles = orbitals.reshape(1, bands, 2, all_cells // LANES, LANES).transpose(0, 3, 1, 2, 4)
    tiles = lax.optimization_barrier(tiles.reshape(all_cells // LANES, rows, LANES))
    blocks = tiles.reshape(count * chunks, chunk_tiles, rows, LANES)
    scale = table_scale(GX)
    turn = jnp.asarray(turn_table(count * rows))
    device = jnp.reshape(me, (1,)).astype(jnp.int32)

    def first(me):
        return 0

    def blocks_for(c, distances, me):
        return send_blocks(me, blocks, [lambda me, d=d: (me ^ d) * chunks + c for d in distances])

    distances = list(range(far, count)) + list(range(1, far))
    late = distances[len(distances) - 1 :]
    sends = [blocks_for(c, [d for d in distances if c == 0 or d not in late], device) for c in range(chunks)]
    own_values = pick(tiles, points, sends[0])
    everyone = lax.all_gather(own_values, "kgrp", axis=0, tiled=False)
    chosen = partner == lax.axis_index("kgrp")
    matched = jnp.sum(jnp.where(chosen[:, None, None, None], everyone, jnp.zeros_like(everyone)), axis=0)
    values = jnp.concatenate([own_values, matched], axis=0)[None]
    over_z = [values] + [hop(values, d, count) for d in range(2, count, 2)]
    (here,) = collect(device, [[(part, first) for part in over_z]])
    there = hop(here, 1, count)
    plane_t = jnp.asarray(plane_table(scale))
    picks = [(there if k % 2 else here, lambda me, i=k // 2: i) for k in order]
    own_coef, src_coef = coefficients(device, picks, turn, [coulomb, plane_t])

    received = []
    for c in range(chunks):
        arrived = {
            d: hop(block, d, count)
            for d, block in zip([d for d in distances if c == 0 or d not in late], sends[c])
        }
        received.append(arrived)

    groups = 2 if bands % 16 == 0 else 1
    line_t = jnp.asarray(line_table(scale, order_back, planes, bands // groups))

    fields = []
    for c in range(chunks):
        arrived = received[c]
        if c:
            arrived.update({d: hop(block, d, count) for d, block in zip(late, blocks_for(c, late, after))})
        here = [(arrived[k], first) if k else (blocks, lambda me, c=c: me * chunks + c) for k in order]
        sent, after = exchange(
            device, here, own_coef, src_coef, coulomb, plane_t, turn, c * chunk_planes, chunk_planes,
            [(at, None) for at in range(count)],
        )
        back = {0: sent[0]}
        for k in distances:
            back[k] = hop(sent[order.index(k)], k, count)
        fields += [(back[k][None], first) for k in order_back]

    factor = 1.0 / (scale * scale * math.sqrt(GX * GY * GZ))
    out = line_pass(device, fields, line_t, factor, rows, groups, count)
    out = out.reshape(bands, all_cells // LANES, 2, LANES).transpose(0, 2, 1, 3)
    return out.reshape(1, bands, 2, all_cells)


def solution(mesh):
    return jax.shard_map(
        body,
        mesh=mesh,
        in_specs=(P("kgrp", "band", None, None), P(), P(), P(None, "band")),
        out_specs=P("kgrp", "band", None, None),
        check_vma=False,
    )
```

```python
import math

import jax
import jax.numpy as jnp
import numpy as np
from jax import lax
from jax.experimental import pallas as pl
from jax.experimental.pallas import tpu as pltpu
from jax.sharding import PartitionSpec as P

GX = 32
GY = 32
GZ = 32
LANES = 128
BF16 = jnp.bfloat16
F32 = jnp.float32
VMEM_BYTES = 24 * 1024 * 1024
FREE = pl.CostEstimate(flops=1, bytes_accessed=1, transcendentals=0)


def round_bf16(values):
    return values.astype(BF16).astype(np.float64)


def table_scale(length):
    cosines = np.cos(2.0 * np.pi * np.arange(length // 4) / length)
    best = (np.inf, 1.0)
    for scale in np.linspace(1.0, 2.0, 8193)[:-1]:
        exact = scale * cosines
        error = float(np.max(np.abs(round_bf16(exact) / exact - 1.0)))
        best = min(best, (error, float(scale)))
    return best[1]


def plane_table(scale):
    cell = np.arange(GY * GZ)
    y, z = cell // GZ, cell % GZ
    turns = (y[:, None] * y[None, :] % GY) / GY + (z[:, None] * z[None, :] % GZ) / GZ
    angle = 2.0 * np.pi * (turns % 1.0)
    return (scale * np.stack([np.cos(angle), np.sin(angle)])).astype(BF16)


def line_table(scale, order, planes, bands):
    count = len(order)
    device = np.arange(count)[:, None, None]
    plane = np.arange(planes)[None, :, None]
    x = planes * (device ^ np.array(order)[None, None, :]) + plane
    kx = np.arange(GX)[None, :, None, None]
    angle = 2.0 * np.pi * (kx * x[:, None] % GX) / GX
    cos_t, sin_t = np.cos(angle), np.sin(angle)
    pair = np.stack([np.stack([cos_t, sin_t], -1), np.stack([-sin_t, cos_t], -1)], 2)
    table = np.zeros((count, bands, GX, 2, planes, count, bands, 2), np.float64)
    for band in range(bands):
        table[:, band, :, :, :, :, band, :] = pair
    return (scale * table).reshape(count, bands * GX * 2, planes * count * bands * 2).astype(BF16)


def turn_table(rows):
    table = np.zeros((rows, rows), np.float32)
    even = np.arange(0, rows, 2)
    table[even, even + 1] = -1.0
    table[even + 1, even] = 1.0
    return table.astype(BF16)


def dot(a, b):
    return jnp.dot(a, b, preferred_element_type=F32)


def pick_kernel(points_ref, tiles_ref, *refs):
    out_ref = refs[-1]
    rows = tiles_ref.shape[1]
    lane = lax.broadcasted_iota(jnp.int32, (rows, LANES), 1)

    @pl.loop(0, out_ref.shape[0])
    def _(group):
        def step(m, total):
            point = points_ref[group * LANES + m]
            tile = tiles_ref[lax.shift_right_logical(point, 7)].astype(F32)
            return jnp.where(lane == m, pltpu.roll(tile, (m - point) & (LANES - 1), 1), total)

        total = lax.fori_loop(0, LANES, step, jnp.zeros((rows, LANES), F32), unroll=128)
        out_ref[group] = total.astype(BF16)


def pick(tiles, points, ahead):
    groups = points.shape[0] // LANES
    rows = tiles.shape[1]
    out = pl.pallas_call(
        pick_kernel,
        in_specs=[pl.BlockSpec(memory_space=pltpu.SMEM), pl.BlockSpec(memory_space=pltpu.VMEM)]
        + [pl.BlockSpec(memory_space=pl.ANY)] * len(ahead),
        out_specs=pl.BlockSpec(memory_space=pltpu.VMEM),
        out_shape=jax.ShapeDtypeStruct((groups, rows, LANES), BF16),
        compiler_params=pltpu.CompilerParams(vmem_limit_bytes=VMEM_BYTES),
        name="pick_points",
    )(points, tiles, *ahead)
    return out


def coef_kernel(picks, inputs, me_ref, *refs):
    arrays, turn_ref, own_ref, src_ref = refs[:inputs], refs[inputs], refs[-2], refs[-1]
    values = [arrays[array][lead(me_ref[0])] for array, lead in picks]
    groups = values[0].shape[0] // 2
    nu = groups * LANES
    own = jnp.concatenate([jnp.concatenate([v[g] for g in range(groups)], axis=1) for v in values], axis=0)
    src = jnp.concatenate([jnp.concatenate([v[groups + g] for g in range(groups)], axis=1) for v in values], axis=0)
    turn = turn_ref[...]
    own_ref[:nu] = own.astype(F32).T.astype(BF16)
    own_ref[nu:] = dot(turn, own).T.astype(BF16)
    src_ref[:, :nu] = -src
    src_ref[:, nu:] = (-dot(turn, src)).astype(BF16)


def coefficients(me, values, turn, held):
    arrays, picks = distinct(values)
    tiles, rows, _ = arrays[0].shape[1:]
    high, nu = len(values) * rows, tiles // 2 * LANES
    return pl.pallas_call(
        lambda *refs: coef_kernel(picks, len(arrays), *refs),
        in_specs=[pl.BlockSpec(memory_space=pltpu.SMEM)] + [pl.BlockSpec(memory_space=pltpu.VMEM)] * (len(arrays) + 1 + len(held)),
        out_shape=(jax.ShapeDtypeStruct((2 * nu, high), BF16), jax.ShapeDtypeStruct((high, 2 * nu), BF16)),
        compiler_params=pltpu.CompilerParams(vmem_limit_bytes=VMEM_BYTES),
        cost_estimate=FREE,
        name="coefficients",
    )(me, *arrays, turn, *held)


def exchange_kernel(first_plane, planes, cells, pairs, inputs, me_ref, *refs):
    arrays = refs[:inputs]
    own_ref, src_ref, coulomb_ref, table_ref, turn_ref = refs[inputs : inputs + 5]
    outs, after_ref, grid_ref, turned_ref = refs[inputs + 5 : -3], refs[-3], refs[-2], refs[-1]
    me = me_ref[0]
    after_ref[0] = me
    nu = coulomb_ref.shape[0]
    rows = arrays[0].shape[2]
    high = len(cells) * rows
    wide = 2 * LANES
    parts = GY * GZ // wide

    @pl.loop(0, planes)
    def _(p):
        down = pl.ds(pl.multiple_of(p * high, high), high)
        for part in range(parts):
            columns = slice(part * wide, (part + 1) * wide)
            tile = (p * parts + part) * 2
            wave = jnp.concatenate(
                [jnp.concatenate([arrays[a][lead(me), tile + t] for a, lead in cells], axis=0) for t in range(2)],
                axis=1,
            )
            density = dot(own_ref[...], wave)
            here = pl.ds(pl.multiple_of((first_plane + p) * GY * GZ + part * wide, wide), wide)
            coulomb = coulomb_ref[:, here].astype(F32)
            weighted = jnp.concatenate(
                [(coulomb * density[:nu]).astype(BF16), (coulomb * density[nu:]).astype(BF16)], axis=0
            )
            field = dot(src_ref[...], weighted).astype(BF16)
            grid_ref[down, columns] = field
            turned_ref[down, columns] = (-dot(turn_ref[...], field)).astype(BF16)

    waves = (dot(grid_ref[...], table_ref[0]) + dot(turned_ref[...], table_ref[1])).astype(BF16)
    side = me % 2
    for p in range(planes):
        for at, (out, half) in enumerate(pairs):
            block = waves[p * high + at * rows : p * high + (at + 1) * rows]
            if half is None:
                outs[out][p] = block
            else:
                outs[out][side ^ half, p] = block


def exchange(me, cells, own, src, coulomb, table, turn, first_plane, planes, pairs):
    arrays, places = distinct(cells)
    rows = arrays[0].shape[2]
    high = len(cells) * rows
    area = GY * GZ
    outs = 1 + max(out for out, _ in pairs)
    halves = () if pairs[0][1] is None else (2,)
    vmem = pl.BlockSpec(memory_space=pltpu.VMEM)
    smem = pl.BlockSpec(memory_space=pltpu.SMEM)
    *sent, after = pl.pallas_call(
        lambda *refs: exchange_kernel(first_plane, planes, places, pairs, len(arrays), *refs),
        in_specs=[smem] + [vmem] * (len(arrays) + 5),
        out_specs=[vmem] * outs + [smem],
        out_shape=[jax.ShapeDtypeStruct(halves + (planes, rows, area), BF16)] * outs
        + [jax.ShapeDtypeStruct((1,), jnp.int32)],
        scratch_shapes=[pltpu.VMEM((planes * high, area), BF16)] * 2,
        compiler_params=pltpu.CompilerParams(vmem_limit_bytes=VMEM_BYTES),
        cost_estimate=FREE,
        name="exchange_planes",
    )(me, *arrays, own, src, coulomb, table, turn)
    return sent, after


def collect_kernel(plan, inputs, me_ref, *refs):
    arrays, outs = refs[:inputs], refs[inputs : inputs + len(plan)]
    buffer, in_sems, out_sems = refs[-3:]
    me = me_ref[0]
    ins, backs = [], []
    for out, picks in enumerate(plan):
        for at, (array, lead) in enumerate(picks):
            n = len(ins)
            ins.append(pltpu.make_async_copy(arrays[array].at[lead(me)], buffer.at[n], in_sems.at[n]))
            backs.append(pltpu.make_async_copy(buffer.at[n], outs[out].at[at], out_sems.at[n]))
    for copy in ins:
        copy.start()
    for copy, back in zip(ins, backs):
        copy.wait()
        back.start()
    for back in backs:
        back.wait()


def distinct(picks):
    arrays, places = [], []
    for array, lead in picks:
        at = next((i for i, a in enumerate(arrays) if a is array), len(arrays))
        if at == len(arrays):
            arrays.append(array)
        places.append((at, lead))
    return arrays, places


def send_kernel(leads, me_ref, blocks_ref, *refs):
    outs, sems = refs[:-1], refs[-1]
    copies = [
        pltpu.make_async_copy(blocks_ref.at[lead(me_ref[0])], out.at[0], sems.at[n])
        for n, (lead, out) in enumerate(zip(leads, outs))
    ]
    for copy in copies:
        copy.start()
    for copy in copies:
        copy.wait()


def send_blocks(me, blocks, leads):
    return pl.pallas_call(
        lambda *refs: send_kernel(leads, *refs),
        in_specs=[pl.BlockSpec(memory_space=pltpu.SMEM), pl.BlockSpec(memory_space=pltpu.VMEM)],
        out_specs=[pl.BlockSpec(memory_space=pltpu.HBM)] * len(leads),
        out_shape=[jax.ShapeDtypeStruct((1,) + blocks.shape[1:], blocks.dtype)] * len(leads),
        scratch_shapes=[pltpu.SemaphoreType.DMA((len(leads),))],
        compiler_params=pltpu.CompilerParams(vmem_limit_bytes=VMEM_BYTES),
        cost_estimate=FREE,
        name="send_blocks",
    )(me, blocks)


def collect(me, wanted):
    arrays, places = distinct([pick for picks in wanted for pick in picks])
    plan, at = [], 0
    for picks in wanted:
        plan.append(places[at : at + len(picks)])
        at += len(picks)
    hbm = pl.BlockSpec(memory_space=pltpu.HBM)
    return pl.pallas_call(
        lambda *refs: collect_kernel(plan, len(arrays), *refs),
        in_specs=[pl.BlockSpec(memory_space=pltpu.SMEM)] + [pl.BlockSpec(memory_space=pl.ANY)] * len(arrays),
        out_specs=[hbm] * len(wanted),
        out_shape=[
            jax.ShapeDtypeStruct((len(picks),) + picks[0][0].shape[1:], picks[0][0].dtype) for picks in wanted
        ],
        scratch_shapes=[
            pltpu.VMEM((len(places),) + arrays[0].shape[1:], arrays[0].dtype),
            pltpu.SemaphoreType.DMA((len(places),)),
            pltpu.SemaphoreType.DMA((len(places),)),
        ],
        compiler_params=pltpu.CompilerParams(vmem_limit_bytes=VMEM_BYTES),
        cost_estimate=FREE,
        name="collect_blocks",
    )(me, *arrays)


def line_kernel(factor, group_rows, count, *refs):
    fields, table_ref, out_ref = refs[1:-2], refs[-2], refs[-1]
    start = pl.multiple_of(pl.program_id(0) * group_rows, group_rows)
    picked = [
        f[p, pl.ds(start, group_rows)]
        for c in range(0, len(fields), count)
        for p in range(fields[c].shape[0])
        for f in fields[c : c + count]
    ]
    lines = dot(table_ref[0], jnp.concatenate(picked, axis=0)) * factor
    lines = lines.astype(BF16)
    for t in range(out_ref.shape[1]):
        tile = lines[:, t * LANES : (t + 1) * LANES]
        out_ref[:, t] = tile.reshape(tile.shape[0] // 2, 2, LANES)


def line_pass(me, fields, table, factor, rows, groups, count):
    area = GY * GZ
    group_rows = rows // groups
    tiles = area // LANES
    height = rows // 2 * GX

    def picked(array, lead):
        return pl.BlockSpec((None,) + array.shape[1:], lambda g, me: (lead(me[0]), 0, 0, 0))

    spec = pltpu.PrefetchScalarGridSpec(
        num_scalar_prefetch=1,
        grid=(groups,),
        in_specs=[picked(*f) for f in fields]
        + [pl.BlockSpec((1,) + table.shape[1:], lambda g, me: (me[0], 0, 0))],
        out_specs=pl.BlockSpec((height // groups, tiles, 2, LANES), lambda g, me: (g, 0, 0, 0)),
    )
    return pl.pallas_call(
        lambda *refs: line_kernel(factor, group_rows, count, *refs),
        grid_spec=spec,
        out_shape=jax.ShapeDtypeStruct((height, tiles, 2, LANES), BF16),
        compiler_params=pltpu.CompilerParams(vmem_limit_bytes=VMEM_BYTES),
        cost_estimate=FREE,
        name="line_pass",
    )(me, *[array for array, _ in fields], table)


def hop(array, distance, count):
    return lax.ppermute(array, "band", [(i, i ^ distance) for i in range(count)])


def body(orbitals, points, partner, coulomb):
    _, bands, _, all_cells = orbitals.shape
    rows = 2 * bands
    count = lax.axis_size("band")
    me = lax.axis_index("band")
    planes = GX // count
    chunks = 2 if planes % 2 == 0 else 1
    chunk_planes = planes // chunks
    plane_tiles = GY * GZ // LANES
    chunk_tiles = chunk_planes * plane_tiles

    far = count // 2
    order = list(dict.fromkeys(k for k in [0, far, 2, 1, far + 1, far + 2, *range(count)] if k < count))
    order_back = [0, 2, far, far + 1, far + 3, *range(far, count), *range(far - 1, 0, -1)]
    order_back = list(dict.fromkeys(k for k in order_back if k < count))

    tiles = orbitals.reshape(1, bands, 2, all_cells // LANES, LANES).transpose(0, 3, 1, 2, 4)
    tiles = lax.optimization_barrier(tiles.reshape(all_cells // LANES, rows, LANES))
    blocks = tiles.reshape(count * chunks, chunk_tiles, rows, LANES)
    scale = table_scale(GX)
    turn = jnp.asarray(turn_table(count * rows))
    device = jnp.reshape(me, (1,)).astype(jnp.int32)

    def first(me):
        return 0

    def blocks_for(c, distances, me):
        return send_blocks(me, blocks, [lambda me, d=d: (me ^ d) * chunks + c for d in distances])

    distances = list(range(far, count)) + list(range(1, far))
    late = distances[len(distances) - 1 :]
    sends = [blocks_for(c, [d for d in distances if c == 0 or d not in late], device) for c in range(chunks)]
    own_values = pick(tiles, points, sends[0])
    everyone = lax.all_gather(own_values, "kgrp", axis=0, tiled=False)
    chosen = partner == lax.axis_index("kgrp")
    matched = jnp.sum(jnp.where(chosen[:, None, None, None], everyone, jnp.zeros_like(everyone)), axis=0)
    values = jnp.concatenate([own_values, matched], axis=0)[None]
    over_z = [values] + [hop(values, d, count) for d in range(2, count, 2)]
    (here,) = collect(device, [[(part, first) for part in over_z]])
    there = hop(here, 1, count)
    plane_t = jnp.asarray(plane_table(scale))
    picks = [(there if k % 2 else here, lambda me, i=k // 2: i) for k in order]
    own_coef, src_coef = coefficients(device, picks, turn, [coulomb, plane_t])

    received = []
    for c in range(chunks):
        arrived = {
            d: hop(block, d, count)
            for d, block in zip([d for d in distances if c == 0 or d not in late], sends[c])
        }
        received.append(arrived)

    groups = 2 if bands % 16 == 0 else 1
    line_t = jnp.asarray(line_table(scale, order_back, planes, bands // groups))

    fields = []
    for c in range(chunks):
        arrived = received[c]
        if c:
            arrived.update({d: hop(block, d, count) for d, block in zip(late, blocks_for(c, late, after))})
        here = [(arrived[k], first) if k else (blocks, lambda me, c=c: me * chunks + c) for k in order]
        sent, after = exchange(
            device, here, own_coef, src_coef, coulomb, plane_t, turn, c * chunk_planes, chunk_planes,
            [(at, None) for at in range(count)],
        )
        back = {0: sent[0]}
        for k in distances:
            back[k] = hop(sent[order.index(k)], k, count)
        fields += [(back[k][None], first) for k in order_back]

    factor = 1.0 / (scale * scale * math.sqrt(GX * GY * GZ))
    out = line_pass(device, fields, line_t, factor, rows, groups, count)
    out = out.reshape(bands, all_cells // LANES, 2, LANES).transpose(0, 2, 1, 3)
    return out.reshape(1, bands, 2, all_cells)


def solution(mesh):
    return jax.shard_map(
        body,
        mesh=mesh,
        in_specs=(P("kgrp", "band", None, None), P(), P(), P(None, "band")),
        out_specs=P("kgrp", "band", None, None),
        check_vma=False,
    )
```

```python
import math

import jax
import jax.numpy as jnp
import numpy as np
from jax import lax
from jax.experimental import pallas as pl
from jax.experimental.pallas import tpu as pltpu
from jax.sharding import PartitionSpec as P

GX = 32
GY = 32
GZ = 32
LANES = 128
BF16 = jnp.bfloat16
F32 = jnp.float32
VMEM_BYTES = 24 * 1024 * 1024
FREE = pl.CostEstimate(flops=1, bytes_accessed=1, transcendentals=0)


def round_bf16(values):
    return values.astype(BF16).astype(np.float64)


def table_scale(length):
    cosines = np.cos(2.0 * np.pi * np.arange(length // 4) / length)
    best = (np.inf, 1.0)
    for scale in np.linspace(1.0, 2.0, 8193)[:-1]:
        exact = scale * cosines
        error = float(np.max(np.abs(round_bf16(exact) / exact - 1.0)))
        best = min(best, (error, float(scale)))
    return best[1]


def plane_table(scale):
    cell = np.arange(GY * GZ)
    y, z = cell // GZ, cell % GZ
    turns = (y[:, None] * y[None, :] % GY) / GY + (z[:, None] * z[None, :] % GZ) / GZ
    angle = 2.0 * np.pi * (turns % 1.0)
    return (scale * np.stack([np.cos(angle), np.sin(angle)])).astype(BF16)


def line_table(scale, order, planes, bands):
    count = len(order)
    device = np.arange(count)[:, None, None]
    plane = np.arange(planes)[None, :, None]
    x = planes * (device ^ np.array(order)[None, None, :]) + plane
    kx = np.arange(GX)[None, :, None, None]
    angle = 2.0 * np.pi * (kx * x[:, None] % GX) / GX
    cos_t, sin_t = np.cos(angle), np.sin(angle)
    pair = np.stack([np.stack([cos_t, sin_t], -1), np.stack([-sin_t, cos_t], -1)], 2)
    table = np.zeros((count, bands, GX, 2, planes, count, bands, 2), np.float64)
    for band in range(bands):
        table[:, band, :, :, :, :, band, :] = pair
    return (scale * table).reshape(count, bands * GX * 2, planes * count * bands * 2).astype(BF16)


def turn_table(rows):
    table = np.zeros((rows, rows), np.float32)
    even = np.arange(0, rows, 2)
    table[even, even + 1] = -1.0
    table[even + 1, even] = 1.0
    return table.astype(BF16)


def dot(a, b):
    return jnp.dot(a, b, preferred_element_type=F32)


def pick_kernel(points_ref, tiles_ref, *refs):
    out_ref = refs[-1]
    rows = tiles_ref.shape[1]
    lane = lax.broadcasted_iota(jnp.int32, (rows, LANES), 1)

    @pl.loop(0, out_ref.shape[0])
    def _(group):
        def step(m, total):
            point = points_ref[group * LANES + m]
            tile = tiles_ref[lax.shift_right_logical(point, 7)].astype(F32)
            return jnp.where(lane == m, pltpu.roll(tile, (m - point) & (LANES - 1), 1), total)

        total = lax.fori_loop(0, LANES, step, jnp.zeros((rows, LANES), F32), unroll=128)
        out_ref[group] = total.astype(BF16)


def pick(tiles, points, ahead):
    groups = points.shape[0] // LANES
    rows = tiles.shape[1]
    out = pl.pallas_call(
        pick_kernel,
        in_specs=[pl.BlockSpec(memory_space=pltpu.SMEM), pl.BlockSpec(memory_space=pltpu.VMEM)]
        + [pl.BlockSpec(memory_space=pl.ANY)] * len(ahead),
        out_specs=pl.BlockSpec(memory_space=pltpu.VMEM),
        out_shape=jax.ShapeDtypeStruct((groups, rows, LANES), BF16),
        compiler_params=pltpu.CompilerParams(vmem_limit_bytes=VMEM_BYTES),
        name="pick_points",
    )(points, tiles, *ahead)
    return out


def coef_kernel(picks, inputs, me_ref, *refs):
    arrays, turn_ref, own_ref, src_ref = refs[:inputs], refs[inputs], refs[-2], refs[-1]
    values = [arrays[array][lead(me_ref[0])] for array, lead in picks]
    groups = values[0].shape[0] // 2
    nu = groups * LANES
    own = jnp.concatenate([jnp.concatenate([v[g] for g in range(groups)], axis=1) for v in values], axis=0)
    src = jnp.concatenate([jnp.concatenate([v[groups + g] for g in range(groups)], axis=1) for v in values], axis=0)
    turn = turn_ref[...]
    own_ref[:nu] = own.astype(F32).T.astype(BF16)
    own_ref[nu:] = dot(turn, own).T.astype(BF16)
    src_ref[:, :nu] = -src
    src_ref[:, nu:] = (-dot(turn, src)).astype(BF16)


def coefficients(me, values, turn, held):
    arrays, picks = distinct(values)
    tiles, rows, _ = arrays[0].shape[1:]
    high, nu = len(values) * rows, tiles // 2 * LANES
    return pl.pallas_call(
        lambda *refs: coef_kernel(picks, len(arrays), *refs),
        in_specs=[pl.BlockSpec(memory_space=pltpu.SMEM)] + [pl.BlockSpec(memory_space=pltpu.VMEM)] * (len(arrays) + 1 + len(held)),
        out_shape=(jax.ShapeDtypeStruct((2 * nu, high), BF16), jax.ShapeDtypeStruct((high, 2 * nu), BF16)),
        compiler_params=pltpu.CompilerParams(vmem_limit_bytes=VMEM_BYTES),
        cost_estimate=FREE,
        name="coefficients",
    )(me, *arrays, turn, *held)


def exchange_kernel(first_plane, planes, cells, pairs, inputs, me_ref, *refs):
    arrays = refs[:inputs]
    own_ref, src_ref, coulomb_ref, table_ref, turn_ref = refs[inputs : inputs + 5]
    outs, after_ref, grid_ref, turned_ref = refs[inputs + 5 : -3], refs[-3], refs[-2], refs[-1]
    me = me_ref[0]
    after_ref[0] = me
    for extra, (array, lead) in zip(outs[len(pairs) :], cells[len(pairs) :]):
        extra[0] = arrays[array][lead(me)]
    cells = cells[: len(pairs)]
    nu = coulomb_ref.shape[0]
    rows = arrays[0].shape[2]
    high = len(cells) * rows
    wide = 2 * LANES
    parts = GY * GZ // wide

    @pl.loop(0, planes)
    def _(p):
        down = pl.ds(pl.multiple_of(p * high, high), high)
        for part in range(parts):
            columns = slice(part * wide, (part + 1) * wide)
            tile = (p * parts + part) * 2
            wave = jnp.concatenate(
                [jnp.concatenate([arrays[a][lead(me), tile + t] for a, lead in cells], axis=0) for t in range(2)],
                axis=1,
            )
            density = dot(own_ref[...], wave)
            here = pl.ds(pl.multiple_of((first_plane + p) * GY * GZ + part * wide, wide), wide)
            coulomb = coulomb_ref[:, here].astype(F32)
            weighted = jnp.concatenate(
                [(coulomb * density[:nu]).astype(BF16), (coulomb * density[nu:]).astype(BF16)], axis=0
            )
            field = dot(src_ref[...], weighted).astype(BF16)
            grid_ref[down, columns] = field
            turned_ref[down, columns] = (-dot(turn_ref[...], field)).astype(BF16)

    waves = (dot(grid_ref[...], table_ref[0]) + dot(turned_ref[...], table_ref[1])).astype(BF16)
    side = me % 2
    for p in range(planes):
        for at, (out, half) in enumerate(pairs):
            block = waves[p * high + at * rows : p * high + (at + 1) * rows]
            if half is None:
                outs[out][p] = block
            else:
                outs[out][side ^ half, p] = block


def exchange(me, cells, own, src, coulomb, table, turn, first_plane, planes, pairs):
    arrays, places = distinct(cells)
    rows = arrays[0].shape[2]
    high = len(pairs) * rows
    area = GY * GZ
    outs = 1 + max(out for out, _ in pairs)
    halves = () if pairs[0][1] is None else (2,)
    vmem = pl.BlockSpec(memory_space=pltpu.VMEM)
    smem = pl.BlockSpec(memory_space=pltpu.SMEM)
    *sent, after = pl.pallas_call(
        lambda *refs: exchange_kernel(first_plane, planes, places, pairs, len(arrays), *refs),
        in_specs=[smem] + [vmem] * (len(arrays) + 5),
        out_specs=[vmem] * (outs + len(cells) - len(pairs)) + [smem],
        out_shape=[jax.ShapeDtypeStruct(halves + (planes, rows, area), BF16)] * outs
        + [jax.ShapeDtypeStruct((1,) + a.shape[1:], BF16) for a, _ in cells[len(pairs) :]]
        + [jax.ShapeDtypeStruct((1,), jnp.int32)],
        scratch_shapes=[pltpu.VMEM((planes * high, area), BF16)] * 2,
        compiler_params=pltpu.CompilerParams(vmem_limit_bytes=VMEM_BYTES),
        cost_estimate=FREE,
        name="exchange_planes",
    )(me, *arrays, own, src, coulomb, table, turn)
    return sent, after


def collect_kernel(plan, inputs, me_ref, *refs):
    arrays, outs = refs[:inputs], refs[inputs : inputs + len(plan)]
    buffer, in_sems, out_sems = refs[-3:]
    me = me_ref[0]
    ins, backs = [], []
    for out, picks in enumerate(plan):
        for at, (array, lead) in enumerate(picks):
            n = len(ins)
            ins.append(pltpu.make_async_copy(arrays[array].at[lead(me)], buffer.at[n], in_sems.at[n]))
            backs.append(pltpu.make_async_copy(buffer.at[n], outs[out].at[at], out_sems.at[n]))
    for copy in ins:
        copy.start()
    for copy, back in zip(ins, backs):
        copy.wait()
        back.start()
    for back in backs:
        back.wait()


def distinct(picks):
    arrays, places = [], []
    for array, lead in picks:
        at = next((i for i, a in enumerate(arrays) if a is array), len(arrays))
        if at == len(arrays):
            arrays.append(array)
        places.append((at, lead))
    return arrays, places


def send_kernel(leads, me_ref, blocks_ref, *refs):
    outs, sems = refs[:-1], refs[-1]
    copies = [
        pltpu.make_async_copy(blocks_ref.at[lead(me_ref[0])], out.at[0], sems.at[n])
        for n, (lead, out) in enumerate(zip(leads, outs))
    ]
    for copy in copies:
        copy.start()
    for copy in copies:
        copy.wait()


def send_blocks(me, blocks, leads):
    return pl.pallas_call(
        lambda *refs: send_kernel(leads, *refs),
        in_specs=[pl.BlockSpec(memory_space=pltpu.SMEM), pl.BlockSpec(memory_space=pltpu.VMEM)],
        out_specs=[pl.BlockSpec(memory_space=pltpu.HBM)] * len(leads),
        out_shape=[jax.ShapeDtypeStruct((1,) + blocks.shape[1:], blocks.dtype)] * len(leads),
        scratch_shapes=[pltpu.SemaphoreType.DMA((len(leads),))],
        compiler_params=pltpu.CompilerParams(vmem_limit_bytes=VMEM_BYTES),
        cost_estimate=FREE,
        name="send_blocks",
    )(me, blocks)


def collect(me, wanted):
    arrays, places = distinct([pick for picks in wanted for pick in picks])
    plan, at = [], 0
    for picks in wanted:
        plan.append(places[at : at + len(picks)])
        at += len(picks)
    hbm = pl.BlockSpec(memory_space=pltpu.HBM)
    return pl.pallas_call(
        lambda *refs: collect_kernel(plan, len(arrays), *refs),
        in_specs=[pl.BlockSpec(memory_space=pltpu.SMEM)] + [pl.BlockSpec(memory_space=pl.ANY)] * len(arrays),
        out_specs=[hbm] * len(wanted),
        out_shape=[
            jax.ShapeDtypeStruct((len(picks),) + picks[0][0].shape[1:], picks[0][0].dtype) for picks in wanted
        ],
        scratch_shapes=[
            pltpu.VMEM((len(places),) + arrays[0].shape[1:], arrays[0].dtype),
            pltpu.SemaphoreType.DMA((len(places),)),
            pltpu.SemaphoreType.DMA((len(places),)),
        ],
        compiler_params=pltpu.CompilerParams(vmem_limit_bytes=VMEM_BYTES),
        cost_estimate=FREE,
        name="collect_blocks",
    )(me, *arrays)


def line_kernel(factor, group_rows, count, *refs):
    fields, table_ref, out_ref = refs[1:-2], refs[-2], refs[-1]
    start = pl.multiple_of(pl.program_id(0) * group_rows, group_rows)
    picked = [
        f[p, pl.ds(start, group_rows)]
        for c in range(0, len(fields), count)
        for p in range(fields[c].shape[0])
        for f in fields[c : c + count]
    ]
    lines = dot(table_ref[0], jnp.concatenate(picked, axis=0)) * factor
    lines = lines.astype(BF16)
    for t in range(out_ref.shape[1]):
        tile = lines[:, t * LANES : (t + 1) * LANES]
        out_ref[:, t] = tile.reshape(tile.shape[0] // 2, 2, LANES)


def line_pass(me, fields, table, factor, rows, groups, count):
    area = GY * GZ
    group_rows = rows // groups
    tiles = area // LANES
    height = rows // 2 * GX

    def picked(array, lead):
        return pl.BlockSpec((None,) + array.shape[1:], lambda g, me: (lead(me[0]), 0, 0, 0))

    spec = pltpu.PrefetchScalarGridSpec(
        num_scalar_prefetch=1,
        grid=(groups,),
        in_specs=[picked(*f) for f in fields]
        + [pl.BlockSpec((1,) + table.shape[1:], lambda g, me: (me[0], 0, 0))],
        out_specs=pl.BlockSpec((height // groups, tiles, 2, LANES), lambda g, me: (g, 0, 0, 0)),
    )
    return pl.pallas_call(
        lambda *refs: line_kernel(factor, group_rows, count, *refs),
        grid_spec=spec,
        out_shape=jax.ShapeDtypeStruct((height, tiles, 2, LANES), BF16),
        compiler_params=pltpu.CompilerParams(vmem_limit_bytes=VMEM_BYTES),
        cost_estimate=FREE,
        name="line_pass",
    )(me, *[array for array, _ in fields], table)


def hop(array, distance, count):
    return lax.ppermute(array, "band", [(i, i ^ distance) for i in range(count)])


def body(orbitals, points, partner, coulomb):
    _, bands, _, all_cells = orbitals.shape
    rows = 2 * bands
    count = lax.axis_size("band")
    me = lax.axis_index("band")
    planes = GX // count
    chunks = 2 if planes % 2 == 0 else 1
    chunk_planes = planes // chunks
    plane_tiles = GY * GZ // LANES
    chunk_tiles = chunk_planes * plane_tiles

    far = count // 2
    order = list(dict.fromkeys(k for k in [0, far, 2, 1, far + 1, far + 2, *range(count)] if k < count))
    order_back = [0, 2, far, far + 1, far + 3, *range(far, count), *range(far - 1, 0, -1)]
    order_back = list(dict.fromkeys(k for k in order_back if k < count))

    tiles = orbitals.reshape(1, bands, 2, all_cells // LANES, LANES).transpose(0, 3, 1, 2, 4)
    tiles = lax.optimization_barrier(tiles.reshape(all_cells // LANES, rows, LANES))
    blocks = tiles.reshape(count * chunks, chunk_tiles, rows, LANES)
    scale = table_scale(GX)
    turn = jnp.asarray(turn_table(count * rows))
    device = jnp.reshape(me, (1,)).astype(jnp.int32)

    def first(me):
        return 0

    def blocks_for(c, distances, me):
        return send_blocks(me, blocks, [lambda me, d=d: (me ^ d) * chunks + c for d in distances])

    distances = list(range(far, count)) + list(range(1, far))
    late = distances[len(distances) - 1 :]
    sends = [blocks_for(c, [d for d in distances if c == 0 or d not in late], device) for c in range(chunks)]
    own_values = pick(tiles, points, sends[0])
    everyone = lax.all_gather(own_values, "kgrp", axis=0, tiled=False)
    chosen = partner == lax.axis_index("kgrp")
    matched = jnp.sum(jnp.where(chosen[:, None, None, None], everyone, jnp.zeros_like(everyone)), axis=0)
    values = jnp.concatenate([own_values, matched], axis=0)[None]
    over_z = [values] + [hop(values, d, count) for d in range(2, count, 2)]
    (here,) = collect(device, [[(part, first) for part in over_z]])
    there = hop(here, 1, count)
    plane_t = jnp.asarray(plane_table(scale))
    picks = [(there if k % 2 else here, lambda me, i=k // 2: i) for k in order]
    own_coef, src_coef = coefficients(device, picks, turn, [coulomb, plane_t])

    received = []
    for c in range(chunks):
        arrived = {
            d: hop(block, d, count)
            for d, block in zip([d for d in distances if c == 0 or d not in late], sends[c])
        }
        received.append(arrived)

    groups = 2 if bands % 16 == 0 else 1
    line_t = jnp.asarray(line_table(scale, order_back, planes, bands // groups))

    fields = []
    for c in range(chunks):
        arrived = received[c]
        if c:
            arrived.update({d: hop(block, d, count) for d, block in zip(late, sent[count:])})
        here = [(arrived[k], first) if k else (blocks, lambda me, c=c: me * chunks + c) for k in order]
        if c < chunks - 1:
            here += [(blocks, lambda me, c=c, d=d: (me ^ d) * chunks + c + 1) for d in late]
        sent, _ = exchange(
            device, here, own_coef, src_coef, coulomb, plane_t, turn, c * chunk_planes, chunk_planes,
            [(at, None) for at in range(count)],
        )
        back = {0: sent[0]}
        for k in distances:
            back[k] = hop(sent[order.index(k)], k, count)
        fields += [(back[k][None], first) for k in order_back]

    factor = 1.0 / (scale * scale * math.sqrt(GX * GY * GZ))
    out = line_pass(device, fields, line_t, factor, rows, groups, count)
    out = out.reshape(bands, all_cells // LANES, 2, LANES).transpose(0, 2, 1, 3)
    return out.reshape(1, bands, 2, all_cells)


def solution(mesh):
    return jax.shard_map(
        body,
        mesh=mesh,
        in_specs=(P("kgrp", "band", None, None), P(), P(), P(None, "band")),
        out_specs=P("kgrp", "band", None, None),
        check_vma=False,
    )
```
